256 devices in a mesh: dp: 16 (over x, y), fsdp: 16 (over z, core).
Axes of the slice: x: 4, y: 4, z: 8, core: 2. Of those that a mesh axis runs over, the one named last changes fastest.
Arguments:
- stream: bfloat16 [131072, 4096], P(('dp', 'fsdp')), may hold values from -6 to 6
- lengths: int32 [256, 2], P(('dp', 'fsdp')), may hold values from 192 to 320, as said below
- partner: int32 [512], P(('dp', 'fsdp')), may hold values from 0 to 511, each once
- norm_gain: bfloat16 [4096], replicated, may hold values from 0.25 to 1.75
- w_query: bfloat16 [4096, 2048], P('fsdp'), may hold values from -0.09375 to 0.09375
- key_weight: bfloat16 [4096, 512], P('fsdp'), may hold values from -0.09375 to 0.09375
- value_weight: bfloat16 [4096, 512], P('fsdp'), may hold values from -0.09375 to 0.09375
- w_out: bfloat16 [2048, 4096], P('fsdp'), may hold values from -0.125 to 0.125
- q_gain: bfloat16 [128], replicated, may hold values from 0.099609375 to 1.8984375
- key_norm_gain: bfloat16 [128], replicated, may hold values from 0.099609375 to 1.8984375
- final_gain: bfloat16 [4096], replicated, may hold values from 0.099609375 to 1.8984375
Outputs:
- embed_grad: float32 [512, 4096], P(('dp', 'fsdp'))
- loss: float32 [], replicated
The draws below stay inside these ranges and needn't reach their ends.
Inputs may be any that keep to these rules, and one draw needn't show every extreme that they name: `lengths`: each device's row sums to 512; some device holds a text of exactly 320 tokens. `partner`: each index appears once.
All inputs are finite; a program needn't handle non-finite values.
Results may differ from the reference program's by a relative error of at most 0.004.
Values may be sent and summed in bfloat16 or wider, within the bound.
A program may use at most 128 MiB of HBM per device.

```python
import math
import jax
import jax.numpy as jnp
from jax import lax

MODEL_WIDTH = 4096
QUERY_HEADS = 16
KEY_VALUE_HEADS = 4
HEAD_SIZE = 128
TOK_DEV = 512
TEXTS_PER_DEVICE = 2
MOST_LEN = 320
TEXTS = 512
TOKENS = 131072
DEVICES = 256


def draw_lengths(key, part):
    key = jax.random.fold_in(key, 1)
    key_long, key_pick, key_flip = jax.random.split(key, 3)
    longer = jax.random.randint(key_long, (DEVICES,), TOK_DEV - MOST_LEN, MOST_LEN + 1).astype(jnp.int32)
    chosen = jax.random.randint(key_pick, (), 0, DEVICES).astype(jnp.int32)
    longer = jnp.where(jnp.arange(DEVICES, dtype=jnp.int32) == chosen, MOST_LEN, longer).astype(jnp.int32)
    flipped = jax.random.randint(key_flip, (DEVICES,), 0, 2).astype(jnp.int32)
    first_len = jnp.where(flipped == 1, longer, TOK_DEV - longer).astype(jnp.int32)
    return jnp.stack([first_len, TOK_DEV - first_len], axis=1).astype(jnp.int32)


def levels(key, shape, pieces, least, high):
    loudness = 1.0
    for position, blocks in pieces:
        draws = jax.random.uniform(jax.random.fold_in(jax.random.fold_in(key, 6), position), (blocks,), jnp.float32, least / len(pieces), high / len(pieces))
        loudness = loudness * jnp.repeat(jnp.exp(draws), shape[position] // blocks).reshape((-1,) + (1,) * (len(shape) - 1 - position))
    return loudness


def centred(key, extent, width, reach, shards=(), held_as=jnp.bfloat16):
    result = jax.random.normal(key, extent, jnp.float32) * width
    if len(shards) > 0:
        result = levels(key, extent, shards, -0.22, 0.18) * result
    return jnp.clip(result, min=-reach, max=reach).astype(held_as)


def setup_inputs(seed: int = 0) -> dict:
    seeds = jax.random.split(jax.random.key(seed), 12)
    stream = centred(seeds[0], (TOKENS, MODEL_WIDTH), 1.0, 6.0, ((0, 256),))
    lengths = draw_lengths(jax.random.fold_in(seeds[11], 71), 0)
    partner = jax.random.permutation(seeds[2], TEXTS).astype(jnp.int32)
    norm_gain = jnp.clip(1.0 + 0.15 * jax.random.normal(seeds[3], (MODEL_WIDTH,), jnp.float32), 0.25, 1.75).astype(jnp.bfloat16)
    w_query = centred(seeds[4], (MODEL_WIDTH, QUERY_HEADS * HEAD_SIZE), MODEL_WIDTH ** -0.5, 0.09375, ((0, 16),))
    key_weight = centred(seeds[5], (MODEL_WIDTH, KEY_VALUE_HEADS * HEAD_SIZE), MODEL_WIDTH ** -0.5, 0.09375, ((0, 16),))
    value_weight = centred(seeds[6], (MODEL_WIDTH, KEY_VALUE_HEADS * HEAD_SIZE), MODEL_WIDTH ** -0.5, 0.09375, ((0, 16),))
    w_out = centred(seeds[7], (QUERY_HEADS * HEAD_SIZE, MODEL_WIDTH), (QUERY_HEADS * HEAD_SIZE) ** -0.5, 0.125, ((0, 16),))
    q_gain = jnp.clip(1.0 + 0.18 * jax.random.normal(seeds[8], (HEAD_SIZE,), jnp.float32), 0.099609375, 1.8984375).astype(jnp.bfloat16)
    key_norm_gain = jnp.clip(1.0 + 0.18 * jax.random.normal(seeds[9], (HEAD_SIZE,), jnp.float32), 0.099609375, 1.8984375).astype(jnp.bfloat16)
    final_gain = jnp.clip(1.0 + 0.18 * jax.random.normal(seeds[10], (MODEL_WIDTH,), jnp.float32), 0.099609375, 1.8984375).astype(jnp.bfloat16)
    return {"stream": stream, "lengths": lengths, "partner": partner, "norm_gain": norm_gain, "w_query": w_query, "key_weight": key_weight, "value_weight": value_weight, "w_out": w_out, "q_gain": q_gain, "key_norm_gain": key_norm_gain, "final_gain": final_gain}


EPS = 1e-06
THETA = 1000000.0
TEMPER = 0.05

def per_head_norm(value_rows, gain):
    square = lax.optimization_barrier(jnp.mean(value_rows * value_rows, axis=-1, keepdims=True))
    return value_rows * lax.rsqrt(square + EPS) * gain.astype(jnp.float32)

def apply_rotary(value_rows, token_position):
    half = value_rows.shape[-1] // 2
    freq = THETA ** (-jnp.arange(half, dtype=jnp.float32) * 2.0 / value_rows.shape[-1])
    angle = token_position.astype(jnp.float32)[:, None, None] * freq[None, None, :]
    cosine = jnp.cos(angle)
    sine = jnp.sin(angle)
    first = value_rows[..., :half]
    second = value_rows[..., half:]
    return jnp.concatenate([first * cosine - second * sine, second * cosine + first * sine], axis=-1)

def layout(lengths, token_count):
    ends = jnp.cumsum(lengths).astype(jnp.int32)
    starts = (ends - lengths).astype(jnp.int32)
    place = jnp.arange(token_count, dtype=jnp.int32)
    member = (place[:, None] >= starts[None, :]) & (place[:, None] < ends[None, :])
    first = lax.optimization_barrier(jnp.sum(jnp.where(member, starts[None, :], 0), axis=1)).astype(jnp.int32)
    return (member, place - first, (ends - 1).astype(jnp.int32))

def embed_block(stream, lengths, norm_gain, w_query, key_weight, value_weight, w_out, q_gain, key_norm_gain, final_gain):
    token_count = stream.shape[0]
    member, token_position, last = layout(lengths, token_count)
    flat = stream.astype(jnp.float32)
    normalized = (flat * lax.rsqrt(lax.optimization_barrier(jnp.mean(flat * flat, axis=-1, keepdims=True)) + EPS) * norm_gain.astype(jnp.float32)).astype(jnp.bfloat16)
    key_rows = jnp.dot(normalized, key_weight, preferred_element_type=jnp.float32).reshape(token_count, KEY_VALUE_HEADS, HEAD_SIZE)
    key_rows = apply_rotary(per_head_norm(key_rows, key_norm_gain), token_position).astype(jnp.bfloat16)
    value_rows = jnp.dot(normalized, value_weight, preferred_element_type=jnp.float32).astype(jnp.bfloat16).reshape(token_count, KEY_VALUE_HEADS, HEAD_SIZE)
    pooled = jnp.take(normalized, last, axis=0)
    query_rows = jnp.dot(pooled, w_query, preferred_element_type=jnp.float32).reshape(TEXTS_PER_DEVICE, QUERY_HEADS, HEAD_SIZE)
    query_rows = apply_rotary(per_head_norm(query_rows, q_gain), lengths - 1).astype(jnp.bfloat16)
    query_rows = query_rows.reshape(TEXTS_PER_DEVICE, KEY_VALUE_HEADS, QUERY_HEADS // KEY_VALUE_HEADS, HEAD_SIZE)
    scores = jnp.einsum('skgd,tkd->skgt', query_rows.astype(jnp.float32), key_rows.astype(jnp.float32)) / math.sqrt(HEAD_SIZE)
    inside = member.T.astype(jnp.float32)[:, None, None, :]
    weights = jnp.exp(scores) * inside
    probs = (weights / lax.optimization_barrier(jnp.sum(weights, axis=-1, keepdims=True))).astype(jnp.bfloat16)
    mixed = jnp.einsum('skgt,tkd->skgd', probs.astype(jnp.float32), value_rows.astype(jnp.float32))
    mixed = mixed.reshape(TEXTS_PER_DEVICE, QUERY_HEADS * HEAD_SIZE).astype(jnp.bfloat16)
    state = jnp.take(stream, last, axis=0).astype(jnp.float32) + jnp.dot(mixed, w_out, preferred_element_type=jnp.float32)
    scaled = state * lax.rsqrt(lax.optimization_barrier(jnp.mean(state * state, axis=-1, keepdims=True)) + EPS) * final_gain.astype(jnp.float32)
    return (scaled / jnp.sqrt(lax.optimization_barrier(jnp.sum(scaled * scaled, axis=-1, keepdims=True)) + EPS)).astype(jnp.bfloat16)

def reference(stream, lengths, partner, norm_gain, w_query, key_weight, value_weight, w_out, q_gain, key_norm_gain, final_gain):
    blocks = stream.reshape(DEVICES, TOK_DEV, MODEL_WIDTH)

    def one_device(item):
        return embed_block(item[0], item[1], norm_gain, w_query, key_weight, value_weight, w_out, q_gain, key_norm_gain, final_gain)
    embedding = lax.map(one_device, (blocks, lengths)).reshape(TEXTS, MODEL_WIDTH)
    scores = jnp.dot(embedding, embedding.T, preferred_element_type=jnp.float32) / TEMPER
    rows = jnp.arange(TEXTS, dtype=jnp.int32)
    hit = rows[None, :] == partner[:, None]
    keep = (rows[None, :] != rows[:, None]) | hit
    weights = jnp.where(keep, jnp.exp(scores), 0.0)
    total = lax.optimization_barrier(jnp.sum(weights, axis=1))
    target = lax.optimization_barrier(jnp.sum(jnp.where(hit, scores, 0.0), axis=1))
    loss = jnp.sum(jnp.log(total) - target) / TEXTS
    pull = (weights / total[:, None] - hit.astype(jnp.float32)).astype(jnp.bfloat16)
    embed_grad = (jnp.dot(pull.T, embedding, preferred_element_type=jnp.float32) + jnp.dot(pull, embedding, preferred_element_type=jnp.float32)) / TEMPER
    return (embed_grad, loss)
```

```python
import functools
import math

import jax
import jax.numpy as jnp
import numpy as np
from jax import lax
from jax.experimental import pallas as pl
from jax.experimental.pallas import tpu as pltpu
from jax.sharding import PartitionSpec as P

QUERY_HEADS = 16
KEY_VALUE_HEADS = 4
HEAD_SIZE = 128
WIDTH = 4096
TOKENS = 512
TEXTS = 512
LEAST_LAST = 191
MOST_LAST = 319
SIDE = 4
ND = 16
NF = 16
COLS = WIDTH // NF

EPS = 1e-06
THETA = 1000000.0
TEMPER = 0.05

F32 = jnp.float32
BF16 = jnp.bfloat16


def rotary_tables():
    half = HEAD_SIZE // 2
    freq = (THETA ** (-np.arange(half, dtype=np.float64) * 2.0 / HEAD_SIZE)).astype(np.float32)
    angle = np.arange(TOKENS, dtype=np.float32)[:, None] * freq[None, :]
    cosine, sine = np.cos(angle), np.sin(angle)
    return (
        np.concatenate([cosine, cosine], axis=1).astype(np.float32),
        np.concatenate([-sine, sine], axis=1).astype(np.float32),
    )


def remote(src, dst, send_sem, recv_sem, device):
    return pltpu.make_async_remote_copy(
        src_ref=src,
        dst_ref=dst,
        send_sem=send_sem,
        recv_sem=recv_sem,
        device_id=device,
        device_id_type=pl.DeviceIdType.MESH,
    )


def wait_bytes(ref, sem):
    pltpu.make_async_copy(ref, ref, sem).wait()


class Place:
    def __init__(self):
        self.d = lax.axis_index("dp")
        self.f = lax.axis_index("fsdp")
        self.x, self.y = self.d // SIDE, self.d % SIDE
        self.z, self.c = self.f // 2, self.f % 2
        self.sibling = (self.d, self.f + 1 - 2 * self.c)

    def index(self, k1, k2):
        xx = lax.rem(self.x + k1 * (1 - self.c) + k2 * self.c, SIDE)
        yy = lax.rem(self.y + k1 * self.c + k2 * (1 - self.c), SIDE)
        return xx * SIDE + yy


class Gather:
    def __init__(self, place, source, piece, block, half, most, whole, seven, sems):
        self.p, self.source, self.piece = place, source, piece
        self.block, self.half, self.most, self.whole, self.seven = block, half, most, whole, seven
        self.s1_send, self.s1_sib, self.s1_recv, self.sends, self.sib_send, self.sib_recv, self.r1, self.r2 = sems
        self.own_half = place.f // (NF // 2)

    def start(self):
        p = self.p
        core = self.own_half
        dst = self.piece(p.f, p.d)

        def one(k, carry):
            z = lax.rem(p.z + k, NF // 2)
            remote(self.source, dst, self.s1_send, self.s1_recv, (p.d, z * 2 + core)).start()
            return carry

        lax.fori_loop(1, NF // 2, one, 0)

        @pl.when(p.c == core)
        def _():
            pltpu.make_async_copy(self.source, dst, self.s1_recv).start()

        @pl.when(p.c != core)
        def _():
            remote(self.source, dst, self.s1_sib, self.s1_recv, p.sibling).start()

    def to_second(self, k1):
        p = self.p
        ref = self.block(p.c, p.index(k1, 0))
        remote(ref, ref, self.sends, self.r2.at[k1, 0], (p.index(0, 1), p.f)).start()
        remote(ref, ref, self.sends, self.r2.at[k1, 1], (p.index(0, 3), p.f)).start()

    def to_sibling(self, k1, k2):
        ref = self.block(self.p.c, self.p.index(k1, k2))
        remote(ref, ref, self.sib_send, self.sib_recv, self.p.sibling).start()

    def own(self):
        p = self.p
        ref = self.block(p.c, p.d)
        wait_bytes(ref, self.s1_recv)
        remote(ref, ref, self.sends, self.r1.at[0], (p.index(1, 0), p.f)).start()
        remote(ref, ref, self.sends, self.r1.at[1], (p.index(3, 0), p.f)).start()
        self.to_second(0)
        self.to_sibling(0, 0)

    def first_near(self):
        p = self.p
        for side, k in ((0, 3), (1, 1)):
            e = p.index(k, 0)
            wait_bytes(self.block(p.c, e), self.r1.at[side])
            ref = self.half(p.c, e, side)
            remote(ref, ref, self.sends, self.r1.at[2 + side], (p.index(4 - k, 0), p.f)).start()
            self.to_second(k)
            self.to_sibling(k, 0)

    def first_far(self):
        p = self.p
        e = p.index(2, 0)
        for side in (0, 1):
            wait_bytes(self.half(p.c, e, side), self.r1.at[2 + side])
        self.to_second(2)
        self.to_sibling(2, 0)

    def second_near(self, k1s=(0, 3, 1, 2)):
        p = self.p
        for k1 in k1s:
            for side, k in ((0, 3), (1, 1)):
                e = p.index(k1, k)
                wait_bytes(self.block(p.c, e), self.r2.at[k1, side])
                ref = self.half(p.c, e, side)
                remote(ref, ref, self.sends, self.r2.at[k1, 2 + side], (p.index(0, 4 - k), p.f)).start()
                self.to_sibling(k1, k)

    def second_far(self):
        p = self.p
        for k1 in (0, 3, 1, 2):
            e = p.index(k1, 2)
            for side in (0, 1):
                wait_bytes(self.half(p.c, e, side), self.r2.at[k1, 2 + side])
            self.to_sibling(k1, 2)

    def finish(self):
        wait_bytes(self.whole(1 - self.p.c), self.sib_recv)

    def drain(self):
        p = self.p
        wait_bytes(self.seven, self.s1_send)

        @pl.when(p.c != self.own_half)
        def _():
            wait_bytes(self.source, self.s1_sib)

        wait_bytes(self.most(p.c), self.sends)
        wait_bytes(self.whole(p.c), self.sib_send)


def all_to_all(place, source, target, send_sem, recv_sem):
    p = place

    def one(k, carry):
        g = lax.rem(p.f + k, NF)
        remote(source(g), target(p.f), send_sem, recv_sem, (p.d, g)).start()
        return carry

    pltpu.make_async_copy(source(p.f), target(p.f), recv_sem).start()
    lax.fori_loop(1, NF, one, 0)


def mean_square(rows):
    return jnp.mean(rows * rows, axis=-1, keepdims=True)


def kernel(
    lengths, partner, stream_hbm, norm_gain, wq_hbm, wk_hbm, wv_hbm, wo_hbm, q_gain, k_gain, final_gain,
    cos_hbm, sin_hbm,
    grad_out, loss_out,
    stream, normed, wk, wv, everyone, wq, wo, cos_t, sin_t,
    pool_send, pool_recv, q_send, q_recv, mix_send, mix_recv, mix_f32,
    ab_send, ab_recv, c_send, c_recv, u_send, keys, values, sim,
    load_sem, pair_sem,
    k1s, k1b, k1r, ks, kbs, kbr, kr1, kr2,
    v1s, v1b, v1r, vs, vbs, vbr, vr1, vr2,
    u1s, u1b, u1r, us, ubs, ubr, ur1, ur2,
):
    p = Place()
    d, f = p.d, p.f
    rows_of = lambda g, n: pl.ds(pl.multiple_of(g * n, n), n)
    lanes_of = lambda g, n: pl.ds(pl.multiple_of(g * n, n), n)

    quarter = TOKENS // 4
    loads = [
        pltpu.make_async_copy(stream_hbm.at[pl.ds(i * quarter, quarter)], stream.at[pl.ds(i * quarter, quarter)], load_sem.at[i])
        for i in range(4)
    ]
    loads += [
        pltpu.make_async_copy(wq_hbm, wq, load_sem.at[4]),
        pltpu.make_async_copy(cos_hbm, cos_t, load_sem.at[5]),
        pltpu.make_async_copy(sin_hbm, sin_t, load_sem.at[6]),
    ]
    for load in loads:
        load.start()

    barrier = pltpu.get_barrier_semaphore()

    def greet(k, carry):
        pl.semaphore_signal(barrier, inc=1, device_id=(d, lax.rem(f + k, NF)), device_id_type=pl.DeviceIdType.MESH)
        pl.semaphore_signal(barrier, inc=1, device_id=(lax.rem(d + k, ND), f), device_id_type=pl.DeviceIdType.MESH)
        return carry

    lax.fori_loop(1, NF, greet, 0)
    pl.semaphore_wait(barrier, NF - 1 + ND - 1)

    def weight_gather(hbm, w, sems):
        return Gather(
            p,
            hbm.at[rows_of(d, 16)],
            lambda g, e: w.at[g, e],
            lambda c, e: w.at[pl.ds(c * 8, 8), e],
            lambda c, e, s: w.at[pl.ds(c * 8 + s * 4, 4), e],
            lambda c: w.at[pl.ds(c * 8, 8), pl.ds(0, 15)],
            lambda c: w.at[pl.ds(c * 8, 8)],
            w.at[0, pl.ds(0, 7)],
            sems,
        )

    k_gather = weight_gather(wk_hbm, wk, (k1s, k1b, k1r, ks, kbs, kbr, kr1, kr2))
    v_gather = weight_gather(wv_hbm, wv, (v1s, v1b, v1r, vs, vbs, vbr, vr1, vr2))
    u_gather = Gather(
        p,
        u_send,
        lambda g, e: everyone.at[e, :, lanes_of(g, COLS)],
        lambda c, e: everyone.at[e, :, lanes_of(c, WIDTH // 2)],
        lambda c, e, s: everyone.at[e, :, lanes_of(c * 2 + s, WIDTH // 4)],
        lambda c: everyone.at[pl.ds(0, 15), :, lanes_of(c, WIDTH // 2)],
        lambda c: everyone.at[:, :, lanes_of(c, WIDTH // 2)],
        everyone.at[0, :, pl.ds(0, 7 * COLS)],
        (u1s, u1b, u1r, us, ubs, ubr, ur1, ur2),
    )

    k_gather.start()

    for load in loads[:4]:
        load.wait()
    last = lengths[0, 0] - 1
    gain = norm_gain[...].astype(F32)
    for t in range(2):
        if t == 0:
            row = jnp.zeros((16, WIDTH), F32)
            for start in range(LEAST_LAST // 16 * 16, MOST_LAST + 1, 16):
                here = lax.broadcasted_iota(jnp.int32, (16, WIDTH), 0) == last - start
                row += jnp.where(here, stream[pl.ds(start, 16), :].astype(F32), 0.0)
            row = jnp.sum(row, axis=0, keepdims=True)
        else:
            row = stream[pl.ds(TOKENS - 16, 16), :].astype(F32)[15:16]
        norm_row = (row * lax.rsqrt(mean_square(row) + EPS) * gain).astype(BF16).astype(F32)
        for g in range(NF):
            for h in range(2):
                lane = g * COLS + h * 128
                pool_send[pl.ds(g * 8 + t * 2 + h, 1), :] = norm_row[:, lane : lane + 128]
                pool_send[pl.ds(g * 8 + 4 + t * 2 + h, 1), :] = row[:, lane : lane + 128]
    all_to_all(
        p, lambda g: pool_send.at[rows_of(g, 8)], lambda g: pool_recv.at[rows_of(g, 8)], pair_sem.at[0], pair_sem.at[1]
    )
    v_gather.start()
    k_gather.own()

    def norm_rows(i, carry):
        rows = pl.ds(pl.multiple_of(i * 32, 32), 32)
        block = stream[rows, :].astype(F32)
        normed[rows, :] = (block * lax.rsqrt(mean_square(block) + EPS) * gain).astype(BF16)
        return carry

    lax.fori_loop(0, TOKENS // 32, norm_rows, 0)

    for load in loads[4:]:
        load.wait()
    wait_bytes(pool_recv, pair_sem.at[1])

    def pooled_block(first):
        return jnp.concatenate(
            [
                jnp.concatenate([pool_recv[pl.ds(first + t * 2 + h, NF, stride=8), :] for h in range(2)], axis=1)
                for t in range(2)
            ],
            axis=0,
        )

    shares = jnp.dot(pooled_block(0).astype(BF16), wq[...], preferred_element_type=F32)
    for t in range(2):
        for h in range(QUERY_HEADS):
            q_send[pl.ds(t * 16 + h, NF, stride=32), :] = shares[t * 16 : t * 16 + 16, h * 128 : h * 128 + 128]
    all_to_all(
        p, lambda g: q_send.at[rows_of(g, 32)], lambda g: q_recv.at[rows_of(g, 32)], pair_sem.at[2], pair_sem.at[3]
    )

    k_gather.first_near()
    k_gather.first_far()
    v_gather.own()
    all_to_all(p, lambda g: wo_hbm.at[:, lanes_of(g, COLS)], lambda g: wo.at[g], pair_sem.at[4], pair_sem.at[5])

    wait_bytes(q_recv, pair_sem.at[3])
    query = q_recv[pl.ds(0, 32), :]
    for g in range(1, NF):
        query += q_recv[pl.ds(g * 32, 32), :]
    query = query * lax.rsqrt(mean_square(query) + EPS) * q_gain[...].astype(F32)
    row32 = lax.broadcasted_iota(jnp.int32, (32, 128), 0)

    def pooled_angle(table):
        start = LEAST_LAST // 8 * 8
        rows = table[pl.ds(start, MOST_LAST + 1 - start), :]
        here = lax.broadcasted_iota(jnp.int32, rows.shape, 0) == last - start
        first = jnp.sum(jnp.where(here, rows, 0.0), axis=0, keepdims=True)
        return jnp.where(row32 < 16, first, table[pl.ds(TOKENS - 1, 1), :])

    query = query * pooled_angle(cos_t) + pltpu.roll(query, 64, 1) * pooled_angle(sin_t)
    group = row32 % 16 // 4
    q_block = jnp.concatenate(
        [jnp.where(group == g, query, 0.0) for g in range(KEY_VALUE_HEADS)], axis=1
    ).astype(BF16)

    k_gather.second_near()
    v_gather.first_near()
    v_gather.first_far()
    k_gather.second_far()
    k_gather.finish()

    key_gain = k_gain[...].astype(F32)

    def key_rows(i, carry):
        rows = pl.ds(pl.multiple_of(i * 128, 128), 128)
        product = jnp.dot(normed[rows, :], wk[...].reshape(WIDTH, 512), preferred_element_type=F32)
        for g in range(KEY_VALUE_HEADS):
            one = product[:, g * 128 : g * 128 + 128]
            one = one * lax.rsqrt(mean_square(one) + EPS) * key_gain
            one = one * cos_t[rows, :] + pltpu.roll(one, 64, 1) * sin_t[rows, :]
            keys[rows, g * 128 : g * 128 + 128] = one.astype(BF16)
        return carry

    lax.fori_loop(0, TOKENS // 128, key_rows, 0)
    scores = lax.dot_general(q_block, keys[...], (((1,), (1,)), ((), ())), preferred_element_type=F32)
    scores = scores * (1.0 / math.sqrt(HEAD_SIZE))
    token = lax.broadcasted_iota(jnp.int32, scores.shape, 1)
    first_text = lax.broadcasted_iota(jnp.int32, scores.shape, 0) < 16
    inside = (token < lengths[0, 0]) == first_text
    weights = jnp.where(inside, jnp.exp(scores), 0.0)
    probs = (weights / jnp.sum(weights, axis=1, keepdims=True)).astype(BF16)

    v_gather.second_near()
    v_gather.second_far()
    v_gather.finish()

    def value_rows(i, carry):
        rows = pl.ds(pl.multiple_of(i * 128, 128), 128)
        values[rows, :] = jnp.dot(
            normed[rows, :], wv[...].reshape(WIDTH, 512), preferred_element_type=F32
        ).astype(BF16)
        return carry

    lax.fori_loop(0, TOKENS // 128, value_rows, 0)
    all_mixed = jnp.dot(probs, values[...], preferred_element_type=F32)
    mixed = jnp.zeros((32, 128), F32)
    for g in range(KEY_VALUE_HEADS):
        mixed += jnp.where(group == g, all_mixed[:, g * 128 : g * 128 + 128], 0.0)
    mix_send[...] = mixed.astype(BF16)
    all_to_all(p, lambda g: mix_send, lambda g: mix_recv.at[g], pair_sem.at[6], pair_sem.at[7])
    wait_bytes(wo, pair_sem.at[5])
    wait_bytes(mix_recv, pair_sem.at[7])

    mix_f32[...] = mix_recv[...].astype(F32).reshape(NF * 32, 128)
    wide = jnp.concatenate(
        [
            jnp.concatenate([mix_f32[pl.ds(t * 16 + h, NF, stride=32), :] for h in range(QUERY_HEADS)], axis=1)
            for t in range(2)
        ],
        axis=0,
    ).astype(BF16)
    state = pooled_block(4) + jnp.dot(wide, wo[...].reshape(2048, COLS), preferred_element_type=F32)
    gained = state * final_gain[:, lanes_of(f, COLS)].astype(F32)
    u_send[...] = gained.astype(BF16)
    u_gather.start()

    offset = d % 4 * 32
    row = lax.broadcasted_iota(jnp.int32, (32, 128), 0)
    lane = lax.broadcasted_iota(jnp.int32, (32, 128), 1)
    diagonal = lane == row + offset
    as_lanes = lambda column: jnp.sum(jnp.where(diagonal, column, 0.0), axis=0, keepdims=True)
    square = as_lanes(jnp.sum(state * state, axis=1, keepdims=True))
    gained_square = as_lanes(jnp.sum(gained * gained, axis=1, keepdims=True))
    lane1 = lax.broadcasted_iota(jnp.int32, (1, 128), 1)
    own = [partner[0, 0], partner[0, 1]]
    partners = jnp.where(lane1 == offset + f, own[0], 0) + jnp.where(lane1 == offset + 16 + f, own[1], 0)
    row8 = lax.broadcasted_iota(jnp.int32, (8, 128), 0)
    pack = lambda parts: functools.reduce(
        lambda total, item: jnp.where(row8 == item[0], item[1], total), enumerate(parts), jnp.zeros((8, 128), F32)
    )
    ab_send[...] = pack([square, gained_square, partners.astype(F32)])
    all_to_all(p, lambda g: ab_send, lambda g: ab_recv.at[rows_of(g, 8)], pair_sem.at[8], pair_sem.at[9])
    u_gather.own()

    wait_bytes(ab_recv, pair_sem.at[9])
    sums = ab_recv[pl.ds(0, 8), :]
    for g in range(1, NF):
        sums += ab_recv[pl.ds(g * 8, 8), :]
    inverse = lax.rsqrt(sums[0:1] / WIDTH + EPS)
    factor = inverse * lax.rsqrt(inverse * inverse * sums[1:2] + EPS)
    factor = jnp.where((lane1 >= offset) & (lane1 < offset + 32), factor, 0.0)
    c_send[...] = pack([factor, sums[2:3]])

    def send_factor(k, carry):
        e = lax.rem(d + k, ND)
        remote(c_send, c_recv.at[rows_of(d, 8)], pair_sem.at[10], pair_sem.at[11], (e, f)).start()
        return carry

    pltpu.make_async_copy(c_send, c_recv.at[rows_of(d, 8)], pair_sem.at[11]).start()
    lax.fori_loop(1, ND, send_factor, 0)

    u_gather.first_near()
    u_gather.first_far()
    u_gather.second_near()
    u_gather.second_far()
    wait_bytes(c_recv, pair_sem.at[11])
    folded = []
    for q in range(4):
        folded.append(sum(c_recv[pl.ds((q * 4 + i) * 8, 8), :] for i in range(1, 4)) + c_recv[pl.ds(q * 32, 8), :])
    factor_row = jnp.concatenate([block[0:1] for block in folded], axis=1)
    partner_row = jnp.concatenate([block[1:2] for block in folded], axis=1).astype(jnp.int32)
    square_row = lax.broadcasted_iota(jnp.int32, (128, 128), 0)
    square_lane = lax.broadcasted_iota(jnp.int32, (128, 128), 1)
    factor_column = [
        jnp.sum(jnp.where(square_row == square_lane, block[0:1], 0.0), axis=1, keepdims=True) for block in folded
    ]
    u_gather.finish()

    name_of = lambda j: j // 32 * 32 + j % 16 * 2 + j % 32 // 16
    total = jnp.zeros((1, TEXTS), F32)
    target = jnp.zeros((1, TEXTS), F32)
    for i in range(4):
        rows = pl.ds(i * 128, 128)
        block = lax.dot_general(
            everyone[pl.ds(i * 4, 4)].reshape(128, WIDTH),
            everyone[...].reshape(TEXTS, WIDTH),
            (((1,), (1,)), ((), ())),
            preferred_element_type=F32,
        )
        block = block * (factor_column[i] * (1.0 / TEMPER)) * factor_row
        sim[rows, :] = block
        i_index = lax.broadcasted_iota(jnp.int32, block.shape, 0) + i * 128
        j_index = lax.broadcasted_iota(jnp.int32, block.shape, 1)
        hit = name_of(i_index) == partner_row
        total += jnp.sum(jnp.where((i_index != j_index) | hit, jnp.exp(block), 0.0), axis=0, keepdims=True)
        target += jnp.sum(jnp.where(hit, block, 0.0), axis=0, keepdims=True)
    loss_out[...] = jnp.sum(jnp.log(total) - target, axis=1, keepdims=True) * (1.0 / TEXTS)

    j_index = lax.broadcasted_iota(jnp.int32, (1, TEXTS), 1)
    names = name_of(j_index)
    coefficient = []
    for t in range(2):
        place = d * 32 + t * 16 + f
        name = (d * NF + f) * 2 + t
        exps = jnp.exp(sim[pl.ds(place, 1), :])
        own_total = jnp.sum(jnp.where(j_index == place, total, 0.0), axis=1, keepdims=True)
        other = j_index != place
        hit = names == own[t]
        back = partner_row == name
        pull = jnp.where(other | hit, exps, 0.0) / own_total - hit.astype(F32)
        pulled = jnp.where(other | back, exps, 0.0) / total - back.astype(F32)
        coefficient.append((pull.astype(BF16).astype(F32) + pulled.astype(BF16).astype(F32)) * factor_row)
    high = [item.astype(BF16).astype(F32) for item in coefficient]
    low = [item - part for item, part in zip(coefficient, high)]
    row16 = lax.broadcasted_iota(jnp.int32, (16, TEXTS), 0)
    stack = jnp.zeros((16, TEXTS), F32)
    for n, item in enumerate(high + low):
        stack = jnp.where(row16 == n, item, stack)
    stack = stack.astype(BF16)
    for n in range(4):
        part = jnp.dot(
            stack,
            everyone[:, :, n * 1024 : n * 1024 + 1024].reshape(TEXTS, 1024),
            preferred_element_type=F32,
        )
        grad_out[:, n * 1024 : n * 1024 + 1024] = (part[0:2] + part[2:4]) * (1.0 / TEMPER)

    for gather in (k_gather, v_gather, u_gather):
        gather.drain()
    wait_bytes(pool_send.at[pl.ds(0, 15 * 8)], pair_sem.at[0])
    wait_bytes(q_send.at[pl.ds(0, 15 * 32)], pair_sem.at[2])
    wait_bytes(wo.at[pl.ds(0, 15)], pair_sem.at[4])
    wait_bytes(mix_recv.at[pl.ds(0, 15)], pair_sem.at[6])
    wait_bytes(ab_recv.at[pl.ds(0, 15 * 8)], pair_sem.at[8])
    wait_bytes(c_recv.at[pl.ds(0, 15 * 8)], pair_sem.at[10])


def local(
    stream, lengths, partner, norm_gain, w_query, key_weight, value_weight, w_out, q_gain, key_norm_gain, final_gain
):
    cos_table, sin_table = rotary_tables()
    vmem = pl.BlockSpec(memory_space=pltpu.VMEM)
    smem = pl.BlockSpec(memory_space=pltpu.SMEM)
    hbm = pl.BlockSpec(memory_space=pltpu.HBM)
    dma = pltpu.SemaphoreType.DMA
    gather_sems = [dma, dma, dma, dma, dma, dma, dma((4,)), dma((4, 4))]
    grad, loss = pl.pallas_call(
        kernel,
        out_shape=(
            jax.ShapeDtypeStruct((2, WIDTH), F32),
            jax.ShapeDtypeStruct((1, 1), F32),
        ),
        in_specs=[smem, smem, hbm, vmem, hbm, hbm, hbm, hbm, vmem, vmem, vmem, hbm, hbm],
        out_specs=(vmem, vmem),
        scratch_shapes=[
            pltpu.VMEM((TOKENS, WIDTH), BF16),
            pltpu.VMEM((TOKENS, WIDTH), BF16),
            pltpu.VMEM((NF, ND, 16, 512), BF16),
            pltpu.VMEM((NF, ND, 16, 512), BF16),
            pltpu.VMEM((ND, 32, WIDTH), BF16),
            pltpu.VMEM((COLS, 2048), BF16),
            pltpu.VMEM((NF, 128, COLS), BF16),
            pltpu.VMEM((TOKENS, HEAD_SIZE), F32),
            pltpu.VMEM((TOKENS, HEAD_SIZE), F32),
            pltpu.VMEM((NF * 8, 128), F32),
            pltpu.VMEM((NF * 8, 128), F32),
            pltpu.VMEM((NF * 32, 128), F32),
            pltpu.VMEM((NF * 32, 128), F32),
            pltpu.VMEM((32, 128), BF16),
            pltpu.VMEM((NF, 32, 128), BF16),
            pltpu.VMEM((NF * 32, 128), F32),
            pltpu.VMEM((8, 128), F32),
            pltpu.VMEM((NF * 8, 128), F32),
            pltpu.VMEM((8, 128), F32),
            pltpu.VMEM((ND * 8, 128), F32),
            pltpu.VMEM((32, COLS), BF16),
            pltpu.VMEM((TOKENS, 512), BF16),
            pltpu.VMEM((TOKENS, 512), BF16),
            pltpu.VMEM((TEXTS, TEXTS), F32),
            dma((7,)),
            dma((12,)),
        ]
        + gather_sems * 3,
        compiler_params=pltpu.CompilerParams(
            collective_id=0, has_side_effects=True, vmem_limit_bytes=60 * 1024 * 1024
        ),
    )(
        lengths,
        partner.reshape(1, 2),
        stream,
        norm_gain.reshape(1, WIDTH),
        w_query,
        key_weight,
        value_weight,
        w_out,
        q_gain.reshape(1, HEAD_SIZE),
        key_norm_gain.reshape(1, HEAD_SIZE),
        final_gain.reshape(1, WIDTH),
        jnp.asarray(cos_table),
        jnp.asarray(sin_table),
    )
    return (grad, loss.reshape(()))


def solution(mesh):
    return jax.shard_map(
        local,
        mesh=mesh,
        in_specs=(
            P(("dp", "fsdp"), None),
            P(("dp", "fsdp"), None),
            P(("dp", "fsdp")),
            P(),
            P("fsdp", None),
            P("fsdp", None),
            P("fsdp", None),
            P("fsdp", None),
            P(),
            P(),
            P(),
        ),
        out_specs=(P(("dp", "fsdp"), None), P()),
        check_vma=False,
    )
```

```python
import functools
import math

import jax
import jax.numpy as jnp
import numpy as np
from jax import lax
from jax.experimental import pallas as pl
from jax.experimental.pallas import tpu as pltpu
from jax.sharding import PartitionSpec as P

QUERY_HEADS = 16
KEY_VALUE_HEADS = 4
HEAD_SIZE = 128
WIDTH = 4096
TOKENS = 512
TEXTS = 512
LEAST_LAST = 191
MOST_LAST = 319
SIDE = 4
ND = 16
NF = 16
COLS = WIDTH // NF

EPS = 1e-06
THETA = 1000000.0
TEMPER = 0.05

F32 = jnp.float32
BF16 = jnp.bfloat16


def rotary_tables():
    half = HEAD_SIZE // 2
    freq = (THETA ** (-np.arange(half, dtype=np.float64) * 2.0 / HEAD_SIZE)).astype(np.float32)
    angle = np.arange(TOKENS, dtype=np.float32)[:, None] * freq[None, :]
    cosine, sine = np.cos(angle), np.sin(angle)
    return (
        np.concatenate([cosine, cosine], axis=1).astype(np.float32),
        np.concatenate([-sine, sine], axis=1).astype(np.float32),
    )


def remote(src, dst, send_sem, recv_sem, device):
    return pltpu.make_async_remote_copy(
        src_ref=src,
        dst_ref=dst,
        send_sem=send_sem,
        recv_sem=recv_sem,
        device_id=device,
        device_id_type=pl.DeviceIdType.MESH,
    )


def wait_bytes(ref, sem):
    pltpu.make_async_copy(ref, ref, sem).wait()


class Place:
    def __init__(self):
        self.d = lax.axis_index("dp")
        self.f = lax.axis_index("fsdp")
        self.x, self.y = self.d // SIDE, self.d % SIDE
        self.z, self.c = self.f // 2, self.f % 2
        self.sibling = (self.d, self.f + 1 - 2 * self.c)

    def index(self, k1, k2):
        xx = lax.rem(self.x + k1 * (1 - self.c) + k2 * self.c, SIDE)
        yy = lax.rem(self.y + k1 * self.c + k2 * (1 - self.c), SIDE)
        return xx * SIDE + yy


class Gather:
    straight = (2,)

    def __init__(self, place, source, piece, block, half, most, whole, seven, sems):
        self.p, self.source, self.piece = place, source, piece
        self.block, self.half, self.most, self.whole, self.seven = block, half, most, whole, seven
        self.s1_send, self.s1_sib, self.s1_recv, self.sends, self.sib_send, self.sib_recv, self.r1, self.r2 = sems
        self.own_half = place.f // (NF // 2)

    def start(self):
        p = self.p
        core = self.own_half
        dst = self.piece(p.f, p.d)

        def one(k, carry):
            z = lax.rem(p.z + k, NF // 2)
            remote(self.source, dst, self.s1_send, self.s1_recv, (p.d, z * 2 + core)).start()
            return carry

        lax.fori_loop(1, NF // 2, one, 0)

        @pl.when(p.c == core)
        def _():
            pltpu.make_async_copy(self.source, dst, self.s1_recv).start()

        @pl.when(p.c != core)
        def _():
            remote(self.source, dst, self.s1_sib, self.s1_recv, p.sibling).start()

    def to_second(self, k1):
        p = self.p
        ref = self.block(p.c, p.index(k1, 0))
        remote(ref, ref, self.sends, self.r2.at[k1, 0], (p.index(0, 1), p.f)).start()
        remote(ref, ref, self.sends, self.r2.at[k1, 1], (p.index(0, 3), p.f)).start()
        if k1 in self.straight:
            remote(ref, ref, self.sends, self.r2.at[k1, 2], (p.index(0, 2), p.f)).start()

    def to_sibling(self, k1, k2):
        ref = self.block(self.p.c, self.p.index(k1, k2))
        remote(ref, ref, self.sib_send, self.sib_recv, self.p.sibling).start()

    def own(self):
        p = self.p
        ref = self.block(p.c, p.d)
        wait_bytes(ref, self.s1_recv)
        remote(ref, ref, self.sends, self.r1.at[0], (p.index(1, 0), p.f)).start()
        remote(ref, ref, self.sends, self.r1.at[1], (p.index(3, 0), p.f)).start()
        remote(ref, ref, self.sends, self.r1.at[2], (p.index(2, 0), p.f)).start()
        self.to_second(0)
        self.to_sibling(0, 0)

    def first_near(self):
        p = self.p
        for side, k in ((0, 3), (1, 1)):
            e = p.index(k, 0)
            wait_bytes(self.block(p.c, e), self.r1.at[side])
            self.to_second(k)
            self.to_sibling(k, 0)

    def first_far(self):
        p = self.p
        e = p.index(2, 0)
        wait_bytes(self.block(p.c, e), self.r1.at[2])
        self.to_second(2)
        self.to_sibling(2, 0)

    def second_near(self, k1s=(0, 3, 1, 2)):
        p = self.p
        for k1 in k1s:
            for side, k in ((0, 3), (1, 1)):
                e = p.index(k1, k)
                wait_bytes(self.block(p.c, e), self.r2.at[k1, side])
                if k1 not in self.straight:
                    ref = self.half(p.c, e, side)
                    remote(ref, ref, self.sends, self.r2.at[k1, 2 + side], (p.index(0, 4 - k), p.f)).start()
                self.to_sibling(k1, k)

    def second_far(self):
        p = self.p
        for k1 in (0, 3, 1, 2):
            e = p.index(k1, 2)
            if k1 in self.straight:
                wait_bytes(self.block(p.c, e), self.r2.at[k1, 2])
            else:
                for side in (0, 1):
                    wait_bytes(self.half(p.c, e, side), self.r2.at[k1, 2 + side])
            self.to_sibling(k1, 2)

    def finish(self):
        wait_bytes(self.whole(1 - self.p.c), self.sib_recv)

    def drain(self):
        p = self.p
        wait_bytes(self.seven, self.s1_send)

        @pl.when(p.c != self.own_half)
        def _():
            wait_bytes(self.source, self.s1_sib)

        wait_bytes(self.most(p.c), self.sends)
        wait_bytes(self.whole(p.c), self.sib_send)


def all_to_all(place, source, target, send_sem, recv_sem):
    p = place

    def one(k, carry):
        g = lax.rem(p.f + k, NF)
        remote(source(g), target(p.f), send_sem, recv_sem, (p.d, g)).start()
        return carry

    pltpu.make_async_copy(source(p.f), target(p.f), recv_sem).start()
    lax.fori_loop(1, NF, one, 0)


def mean_square(rows):
    return jnp.mean(rows * rows, axis=-1, keepdims=True)


def kernel(
    lengths, partner, stream_hbm, norm_gain, wq_hbm, wk_hbm, wv_hbm, wo_hbm, q_gain, k_gain, final_gain,
    cos_hbm, sin_hbm,
    grad_out, loss_out,
    stream, normed, wk, wv, everyone, wq, wo, cos_t, sin_t,
    pool_send, pool_recv, q_send, q_recv, mix_send, mix_recv, mix_f32,
    ab_send, ab_recv, c_send, c_recv, u_send, keys, values, sim,
    load_sem, pair_sem,
    k1s, k1b, k1r, ks, kbs, kbr, kr1, kr2,
    v1s, v1b, v1r, vs, vbs, vbr, vr1, vr2,
    u1s, u1b, u1r, us, ubs, ubr, ur1, ur2,
):
    p = Place()
    d, f = p.d, p.f
    rows_of = lambda g, n: pl.ds(pl.multiple_of(g * n, n), n)
    lanes_of = lambda g, n: pl.ds(pl.multiple_of(g * n, n), n)

    quarter = TOKENS // 4
    loads = [
        pltpu.make_async_copy(stream_hbm.at[pl.ds(i * quarter, quarter)], stream.at[pl.ds(i * quarter, quarter)], load_sem.at[i])
        for i in range(4)
    ]
    loads += [
        pltpu.make_async_copy(wq_hbm, wq, load_sem.at[4]),
        pltpu.make_async_copy(cos_hbm, cos_t, load_sem.at[5]),
        pltpu.make_async_copy(sin_hbm, sin_t, load_sem.at[6]),
    ]
    for load in loads:
        load.start()

    barrier = pltpu.get_barrier_semaphore()

    def greet(k, carry):
        pl.semaphore_signal(barrier, inc=1, device_id=(d, lax.rem(f + k, NF)), device_id_type=pl.DeviceIdType.MESH)
        pl.semaphore_signal(barrier, inc=1, device_id=(lax.rem(d + k, ND), f), device_id_type=pl.DeviceIdType.MESH)
        return carry

    lax.fori_loop(1, NF, greet, 0)
    pl.semaphore_wait(barrier, NF - 1 + ND - 1)

    def weight_gather(hbm, w, sems):
        return Gather(
            p,
            hbm.at[rows_of(d, 16)],
            lambda g, e: w.at[g, e],
            lambda c, e: w.at[pl.ds(c * 8, 8), e],
            lambda c, e, s: w.at[pl.ds(c * 8 + s * 4, 4), e],
            lambda c: w.at[pl.ds(c * 8, 8), pl.ds(0, 15)],
            lambda c: w.at[pl.ds(c * 8, 8)],
            w.at[0, pl.ds(0, 7)],
            sems,
        )

    k_gather = weight_gather(wk_hbm, wk, (k1s, k1b, k1r, ks, kbs, kbr, kr1, kr2))
    v_gather = weight_gather(wv_hbm, wv, (v1s, v1b, v1r, vs, vbs, vbr, vr1, vr2))
    u_gather = Gather(
        p,
        u_send,
        lambda g, e: everyone.at[e, :, lanes_of(g, COLS)],
        lambda c, e: everyone.at[e, :, lanes_of(c, WIDTH // 2)],
        lambda c, e, s: everyone.at[e, :, lanes_of(c * 2 + s, WIDTH // 4)],
        lambda c: everyone.at[pl.ds(0, 15), :, lanes_of(c, WIDTH // 2)],
        lambda c: everyone.at[:, :, lanes_of(c, WIDTH // 2)],
        everyone.at[0, :, pl.ds(0, 7 * COLS)],
        (u1s, u1b, u1r, us, ubs, ubr, ur1, ur2),
    )

    k_gather.start()

    for load in loads[:4]:
        load.wait()
    last = lengths[0, 0] - 1
    gain = norm_gain[...].astype(F32).reshape(1, WIDTH)
    for t in range(2):
        if t == 0:
            row = jnp.zeros((16, WIDTH), F32)
            for start in range(LEAST_LAST // 16 * 16, MOST_LAST + 1, 16):
                here = lax.broadcasted_iota(jnp.int32, (16, WIDTH), 0) == last - start
                row += jnp.where(here, stream[pl.ds(start, 16), :].astype(F32), 0.0)
            row = jnp.sum(row, axis=0, keepdims=True)
        else:
            row = stream[pl.ds(TOKENS - 16, 16), :].astype(F32)[15:16]
        norm_row = (row * lax.rsqrt(mean_square(row) + EPS) * gain).astype(BF16).astype(F32)
        for g in range(NF):
            for h in range(2):
                lane = g * COLS + h * 128
                pool_send[pl.ds(g * 8 + t * 2 + h, 1), :] = norm_row[:, lane : lane + 128]
                pool_send[pl.ds(g * 8 + 4 + t * 2 + h, 1), :] = row[:, lane : lane + 128]
    all_to_all(
        p, lambda g: pool_send.at[rows_of(g, 8)], lambda g: pool_recv.at[rows_of(g, 8)], pair_sem.at[0], pair_sem.at[1]
    )
    v_gather.start()
    k_gather.own()

    def norm_rows(i, carry):
        rows = pl.ds(pl.multiple_of(i * 32, 32), 32)
        block = stream[rows, :].astype(F32)
        normed[rows, :] = (block * lax.rsqrt(mean_square(block) + EPS) * gain).astype(BF16)
        return carry

    lax.fori_loop(0, TOKENS // 32, norm_rows, 0)

    for load in loads[4:]:
        load.wait()
    wait_bytes(pool_recv, pair_sem.at[1])

    def pooled_block(first):
        return jnp.concatenate(
            [
                jnp.concatenate([pool_recv[pl.ds(first + t * 2 + h, NF, stride=8), :] for h in range(2)], axis=1)
                for t in range(2)
            ],
            axis=0,
        )

    shares = jnp.dot(pooled_block(0).astype(BF16), wq[...], preferred_element_type=F32)
    for t in range(2):
        for h in range(QUERY_HEADS):
            q_send[pl.ds(t * 16 + h, NF, stride=32), :] = shares[t * 16 : t * 16 + 16, h * 128 : h * 128 + 128]
    all_to_all(
        p, lambda g: q_send.at[rows_of(g, 32)], lambda g: q_recv.at[rows_of(g, 32)], pair_sem.at[2], pair_sem.at[3]
    )

    k_gather.first_near()
    k_gather.first_far()
    v_gather.own()
    def wo_rows(core):
        return pl.ds(pl.multiple_of((p.x * (1 - core) + p.y * core) * 32, 32), 32)

    def send_wo(k, carry):
        g = lax.rem(f + k, NF)
        rows = wo_rows(g % 2)
        remote(wo_hbm.at[rows, lanes_of(g, COLS)], wo.at[f, rows], pair_sem.at[4], pair_sem.at[5], (d, g)).start()
        return carry

    pltpu.make_async_copy(wo_hbm.at[wo_rows(p.c), lanes_of(f, COLS)], wo.at[f, wo_rows(p.c)], pair_sem.at[5]).start()
    lax.fori_loop(1, NF, send_wo, 0)

    wait_bytes(q_recv, pair_sem.at[3])
    query = q_recv[pl.ds(0, 32), :]
    for g in range(1, NF):
        query += q_recv[pl.ds(g * 32, 32), :]
    query = query * lax.rsqrt(mean_square(query) + EPS) * q_gain[...].astype(F32)
    row32 = lax.broadcasted_iota(jnp.int32, (32, 128), 0)

    def pooled_angle(table):
        start = LEAST_LAST // 8 * 8
        rows = table[pl.ds(start, MOST_LAST + 1 - start), :]
        here = lax.broadcasted_iota(jnp.int32, rows.shape, 0) == last - start
        first = jnp.sum(jnp.where(here, rows, 0.0), axis=0, keepdims=True)
        return jnp.where(row32 < 16, first, table[pl.ds(TOKENS - 1, 1), :])

    query = query * pooled_angle(cos_t) + pltpu.roll(query, 64, 1) * pooled_angle(sin_t)
    group = row32 % 16 // 4
    q_block = jnp.concatenate(
        [jnp.where(group == g, query, 0.0) for g in range(KEY_VALUE_HEADS)], axis=1
    ).astype(BF16)

    k_gather.second_near()
    v_gather.first_near()
    v_gather.first_far()
    k_gather.second_far()

    key_gain = k_gain[...].astype(F32)

    def half_product(w, core, rows):
        return jnp.dot(
            normed[rows, lanes_of(core, WIDTH // 2)],
            w[pl.ds(core * 8, 8)].reshape(WIDTH // 2, 512),
            preferred_element_type=F32,
        )

    def first_half(w):
        for i in range(2):
            rows = pl.ds(i * 256, 256)
            sim[rows, :] = half_product(w, p.c, rows)

    first_half(wk)
    k_gather.finish()
    for i in range(2):
        rows = pl.ds(i * 256, 256)
        sim[rows, :] += half_product(wk, 1 - p.c, rows)
    v_gather.second_near((0,))

    def key_rows(i, carry):
        rows = pl.ds(pl.multiple_of(i * 128, 128), 128)
        for g in range(KEY_VALUE_HEADS):
            one = sim[rows, g * 128 : g * 128 + 128]
            one = one * lax.rsqrt(mean_square(one) + EPS) * key_gain
            one = one * cos_t[rows, :] + pltpu.roll(one, 64, 1) * sin_t[rows, :]
            keys[rows, g * 128 : g * 128 + 128] = one.astype(BF16)
        return carry

    lax.fori_loop(0, TOKENS // 128, key_rows, 0)
    scores = lax.dot_general(q_block, keys[...], (((1,), (1,)), ((), ())), preferred_element_type=F32)
    scores = scores * (1.0 / math.sqrt(HEAD_SIZE))
    token = lax.broadcasted_iota(jnp.int32, scores.shape, 1)
    first_text = lax.broadcasted_iota(jnp.int32, scores.shape, 0) < 16
    inside = (token < lengths[0, 0]) == first_text
    weights = jnp.where(inside, jnp.exp(scores), 0.0)
    probs = (weights / jnp.sum(weights, axis=1, keepdims=True)).astype(BF16)

    v_gather.second_near((3, 1, 2))
    v_gather.second_far()
    own_wo = wo.at[:, wo_rows(p.c)]
    wait_bytes(own_wo, pair_sem.at[5])
    for k in (1, 3, 2):
        remote(own_wo, own_wo, pair_sem.at[12], pair_sem.at[13], (p.index(k, 0), f)).start()

    first_half(wv)
    v_gather.finish()
    for i in range(2):
        rows = pl.ds(i * 256, 256)
        values[rows, :] = (sim[rows, :] + half_product(wv, 1 - p.c, rows)).astype(BF16)
    all_mixed = jnp.dot(probs, values[...], preferred_element_type=F32)
    mixed = jnp.zeros((32, 128), F32)
    for g in range(KEY_VALUE_HEADS):
        mixed += jnp.where(group == g, all_mixed[:, g * 128 : g * 128 + 128], 0.0)
    mix_send[...] = mixed.astype(BF16)
    all_to_all(p, lambda g: mix_send, lambda g: mix_recv.at[g], pair_sem.at[6], pair_sem.at[7])
    wait_bytes(wo.at[pl.ds(0, 12)], pair_sem.at[13])
    wait_bytes(mix_recv, pair_sem.at[7])

    mix_f32[...] = mix_recv[...].astype(F32).reshape(NF * 32, 128)
    wide = jnp.concatenate(
        [
            jnp.concatenate([mix_f32[pl.ds(t * 16 + h, NF, stride=32), :] for h in range(QUERY_HEADS)], axis=1)
            for t in range(2)
        ],
        axis=0,
    ).astype(BF16)
    state = pooled_block(4) + jnp.dot(wide, wo[...].reshape(2048, COLS), preferred_element_type=F32)
    gained = state * final_gain[lanes_of(f, COLS)].astype(F32).reshape(1, COLS)
    u_send[...] = gained.astype(BF16)
    u_gather.start()

    offset = d % 4 * 32
    row = lax.broadcasted_iota(jnp.int32, (32, 128), 0)
    lane = lax.broadcasted_iota(jnp.int32, (32, 128), 1)
    diagonal = lane == row + offset
    as_lanes = lambda column: jnp.sum(jnp.where(diagonal, column, 0.0), axis=0, keepdims=True)
    square = as_lanes(jnp.sum(state * state, axis=1, keepdims=True))
    gained_square = as_lanes(jnp.sum(gained * gained, axis=1, keepdims=True))
    lane1 = lax.broadcasted_iota(jnp.int32, (1, 128), 1)
    own = [partner[0, 0], partner[0, 1]]
    partners = jnp.where(lane1 == offset + f, own[0], 0) + jnp.where(lane1 == offset + 16 + f, own[1], 0)
    row8 = lax.broadcasted_iota(jnp.int32, (8, 128), 0)
    pack = lambda parts: functools.reduce(
        lambda total, item: jnp.where(row8 == item[0], item[1], total), enumerate(parts), jnp.zeros((8, 128), F32)
    )
    ab_send[...] = pack([square, gained_square, partners.astype(F32)])
    all_to_all(p, lambda g: ab_send, lambda g: ab_recv.at[rows_of(g, 8)], pair_sem.at[8], pair_sem.at[9])
    u_gather.own()

    wait_bytes(ab_recv, pair_sem.at[9])
    sums = ab_recv[pl.ds(0, 8), :]
    for g in range(1, NF):
        sums += ab_recv[pl.ds(g * 8, 8), :]
    inverse = lax.rsqrt(sums[0:1] / WIDTH + EPS)
    factor = inverse * lax.rsqrt(inverse * inverse * sums[1:2] + EPS)
    factor = jnp.where((lane1 >= offset) & (lane1 < offset + 32), factor, 0.0)
    c_send[...] = pack([factor, sums[2:3]])

    def send_factor(k, carry):
        e = lax.rem(d + k, ND)
        remote(c_send, c_recv.at[rows_of(d, 8)], pair_sem.at[10], pair_sem.at[11], (e, f)).start()
        return carry

    pltpu.make_async_copy(c_send, c_recv.at[rows_of(d, 8)], pair_sem.at[11]).start()
    lax.fori_loop(1, ND, send_factor, 0)

    u_gather.first_near()
    u_gather.first_far()
    u_gather.second_near()
    u_gather.second_far()
    wait_bytes(c_recv, pair_sem.at[11])
    folded = []
    for q in range(4):
        folded.append(sum(c_recv[pl.ds((q * 4 + i) * 8, 8), :] for i in range(1, 4)) + c_recv[pl.ds(q * 32, 8), :])
    factor_row = jnp.concatenate([block[0:1] for block in folded], axis=1)
    partner_row = jnp.concatenate([block[1:2] for block in folded], axis=1).astype(jnp.int32)
    square_row = lax.broadcasted_iota(jnp.int32, (128, 128), 0)
    square_lane = lax.broadcasted_iota(jnp.int32, (128, 128), 1)
    factor_column = [
        jnp.sum(jnp.where(square_row == square_lane, block[0:1], 0.0), axis=1, keepdims=True) for block in folded
    ]

    def half_scores(core, i):
        return lax.dot_general(
            everyone[pl.ds(i * 8, 8), :, lanes_of(core, WIDTH // 2)].reshape(256, WIDTH // 2),
            everyone[:, :, lanes_of(core, WIDTH // 2)].reshape(TEXTS, WIDTH // 2),
            (((1,), (1,)), ((), ())),
            preferred_element_type=F32,
        )

    for i in range(2):
        sim[pl.ds(i * 256, 256), :] = half_scores(p.c, i)
    u_gather.finish()
    name_of = lambda j: j // 32 * 32 + j % 16 * 2 + j % 32 // 16
    total = jnp.zeros((1, TEXTS), F32)
    target = jnp.zeros((1, TEXTS), F32)
    for i in range(2):
        rows = pl.ds(i * 256, 256)
        block = sim[rows, :] + half_scores(1 - p.c, i)
        column = jnp.concatenate(factor_column[i * 2 : i * 2 + 2], axis=0) * (1.0 / TEMPER)
        block = block * column * factor_row
        sim[rows, :] = block
        i_index = lax.broadcasted_iota(jnp.int32, block.shape, 0) + i * 256
        j_index = lax.broadcasted_iota(jnp.int32, block.shape, 1)
        hit = name_of(i_index) == partner_row
        total += jnp.sum(jnp.where((i_index != j_index) | hit, jnp.exp(block), 0.0), axis=0, keepdims=True)
        target += jnp.sum(jnp.where(hit, block, 0.0), axis=0, keepdims=True)
    loss_out[...] = jnp.sum(jnp.log(total) - target, axis=1, keepdims=True) * (1.0 / TEXTS)

    j_index = lax.broadcasted_iota(jnp.int32, (1, TEXTS), 1)
    names = name_of(j_index)
    coefficient = []
    for t in range(2):
        place = d * 32 + t * 16 + f
        name = (d * NF + f) * 2 + t
        exps = jnp.exp(sim[pl.ds(place, 1), :])
        own_total = jnp.sum(jnp.where(j_index == place, total, 0.0), axis=1, keepdims=True)
        other = j_index != place
        hit = names == own[t]
        back = partner_row == name
        pull = jnp.where(other | hit, exps, 0.0) / own_total - hit.astype(F32)
        pulled = jnp.where(other | back, exps, 0.0) / total - back.astype(F32)
        coefficient.append((pull.astype(BF16).astype(F32) + pulled.astype(BF16).astype(F32)) * factor_row)
    high = [item.astype(BF16).astype(F32) for item in coefficient]
    low = [item - part for item, part in zip(coefficient, high)]
    row16 = lax.broadcasted_iota(jnp.int32, (16, TEXTS), 0)
    stack = jnp.zeros((16, TEXTS), F32)
    for n, item in enumerate(high + low):
        stack = jnp.where(row16 == n, item, stack)
    stack = stack.astype(BF16)
    for n in range(4):
        part = jnp.dot(
            stack,
            everyone[:, :, n * 1024 : n * 1024 + 1024].reshape(TEXTS, 1024),
            preferred_element_type=F32,
        )
        grad_out[:, n * 1024 : n * 1024 + 1024] = (part[0:2] + part[2:4]) * (1.0 / TEMPER)

    for gather in (k_gather, v_gather, u_gather):
        gather.drain()
    wait_bytes(pool_send.at[pl.ds(0, 15 * 8)], pair_sem.at[0])
    wait_bytes(q_send.at[pl.ds(0, 15 * 32)], pair_sem.at[2])
    wait_bytes(wo.at[pl.ds(0, 15), pl.ds(0, 32)], pair_sem.at[4])
    wait_bytes(wo.at[pl.ds(0, 12)], pair_sem.at[12])
    wait_bytes(mix_recv.at[pl.ds(0, 15)], pair_sem.at[6])
    wait_bytes(ab_recv.at[pl.ds(0, 15 * 8)], pair_sem.at[8])
    wait_bytes(c_recv.at[pl.ds(0, 15 * 8)], pair_sem.at[10])


def local(
    stream, lengths, partner, norm_gain, w_query, key_weight, value_weight, w_out, q_gain, key_norm_gain, final_gain
):
    cos_table, sin_table = rotary_tables()
    vmem = pl.BlockSpec(memory_space=pltpu.VMEM)
    smem = pl.BlockSpec(memory_space=pltpu.SMEM)
    hbm = pl.BlockSpec(memory_space=pltpu.HBM)
    dma = pltpu.SemaphoreType.DMA
    gather_sems = [dma, dma, dma, dma, dma, dma, dma((4,)), dma((4, 4))]
    grad, loss = pl.pallas_call(
        kernel,
        out_shape=(
            jax.ShapeDtypeStruct((2, WIDTH), F32),
            jax.ShapeDtypeStruct((1, 1), F32),
        ),
        in_specs=[smem, smem, hbm, vmem, hbm, hbm, hbm, hbm, vmem, vmem, vmem, hbm, hbm],
        out_specs=(vmem, vmem),
        scratch_shapes=[
            pltpu.VMEM((TOKENS, WIDTH), BF16),
            pltpu.VMEM((TOKENS, WIDTH), BF16),
            pltpu.VMEM((NF, ND, 16, 512), BF16),
            pltpu.VMEM((NF, ND, 16, 512), BF16),
            pltpu.VMEM((ND, 32, WIDTH), BF16),
            pltpu.VMEM((COLS, 2048), BF16),
            pltpu.VMEM((NF, 128, COLS), BF16),
            pltpu.VMEM((TOKENS, HEAD_SIZE), F32),
            pltpu.VMEM((TOKENS, HEAD_SIZE), F32),
            pltpu.VMEM((NF * 8, 128), F32),
            pltpu.VMEM((NF * 8, 128), F32),
            pltpu.VMEM((NF * 32, 128), F32),
            pltpu.VMEM((NF * 32, 128), F32),
            pltpu.VMEM((32, 128), BF16),
            pltpu.VMEM((NF, 32, 128), BF16),
            pltpu.VMEM((NF * 32, 128), F32),
            pltpu.VMEM((8, 128), F32),
            pltpu.VMEM((NF * 8, 128), F32),
            pltpu.VMEM((8, 128), F32),
            pltpu.VMEM((ND * 8, 128), F32),
            pltpu.VMEM((32, COLS), BF16),
            pltpu.VMEM((TOKENS, 512), BF16),
            pltpu.VMEM((TOKENS, 512), BF16),
            pltpu.VMEM((TEXTS, TEXTS), F32),
            dma((7,)),
            dma((14,)),
        ]
        + gather_sems * 3,
        compiler_params=pltpu.CompilerParams(
            collective_id=0, has_side_effects=True, vmem_limit_bytes=60 * 1024 * 1024
        ),
    )(
        lengths,
        partner.reshape(1, 2),
        stream,
        norm_gain,
        w_query,
        key_weight,
        value_weight,
        w_out,
        q_gain.reshape(1, HEAD_SIZE),
        key_norm_gain.reshape(1, HEAD_SIZE),
        final_gain,
        jnp.asarray(cos_table),
        jnp.asarray(sin_table),
    )
    return (grad, loss.reshape(()))


def solution(mesh):
    return jax.shard_map(
        local,
        mesh=mesh,
        in_specs=(
            P(("dp", "fsdp"), None),
            P(("dp", "fsdp"), None),
            P(("dp", "fsdp")),
            P(),
            P("fsdp", None),
            P("fsdp", None),
            P("fsdp", None),
            P("fsdp", None),
            P(),
            P(),
            P(),
        ),
        out_specs=(P(("dp", "fsdp"), None), P()),
        check_vma=False,
    )
```

```python
import functools
import math

import jax
import jax.numpy as jnp
import numpy as np
from jax import lax
from jax.experimental import pallas as pl
from jax.experimental.pallas import tpu as pltpu
from jax.sharding import PartitionSpec as P

QUERY_HEADS = 16
KEY_VALUE_HEADS = 4
HEAD_SIZE = 128
WIDTH = 4096
TOKENS = 512
TEXTS = 512
LEAST_LAST = 191
MOST_LAST = 319
K_STRAIGHT = (2,)
V_STRAIGHT = ()
U_STRAIGHT = ()
SIDE = 4
ND = 16
NF = 16
COLS = WIDTH // NF

EPS = 1e-06
THETA = 1000000.0
TEMPER = 0.05

F32 = jnp.float32
BF16 = jnp.bfloat16


def rotary_tables():
    half = HEAD_SIZE // 2
    freq = (THETA ** (-np.arange(half, dtype=np.float64) * 2.0 / HEAD_SIZE)).astype(np.float32)
    angle = np.arange(TOKENS, dtype=np.float32)[:, None] * freq[None, :]
    cosine, sine = np.cos(angle), np.sin(angle)
    return (
        np.concatenate([cosine, cosine], axis=1).astype(np.float32),
        np.concatenate([-sine, sine], axis=1).astype(np.float32),
    )


def remote(src, dst, send_sem, recv_sem, device):
    return pltpu.make_async_remote_copy(
        src_ref=src,
        dst_ref=dst,
        send_sem=send_sem,
        recv_sem=recv_sem,
        device_id=device,
        device_id_type=pl.DeviceIdType.MESH,
    )


def wait_bytes(ref, sem):
    pltpu.make_async_copy(ref, ref, sem).wait()


class Place:
    def __init__(self):
        self.d = lax.axis_index("dp")
        self.f = lax.axis_index("fsdp")
        self.x, self.y = self.d // SIDE, self.d % SIDE
        self.z, self.c = self.f // 2, self.f % 2
        self.sibling = (self.d, self.f + 1 - 2 * self.c)

    def index(self, k1, k2):
        xx = lax.rem(self.x + k1 * (1 - self.c) + k2 * self.c, SIDE)
        yy = lax.rem(self.y + k1 * self.c + k2 * (1 - self.c), SIDE)
        return xx * SIDE + yy


class Gather:
    def __init__(self, place, block, half, most, straight, sems):
        self.p, self.block, self.half, self.most, self.straight = place, block, half, most, straight
        self.sends, self.sib_send, self.sib_recv, self.r1, self.r2 = sems

    def to_second(self, k1):
        p = self.p
        ref = self.block(p.index(k1, 0))
        remote(ref, ref, self.sends, self.r2.at[k1, 0], (p.index(0, 1), p.f)).start()
        remote(ref, ref, self.sends, self.r2.at[k1, 1], (p.index(0, 3), p.f)).start()
        if k1 in self.straight:
            remote(ref, ref, self.sends, self.r2.at[k1, 2], (p.index(0, 2), p.f)).start()

    def to_sibling(self, ref):
        remote(ref, ref, self.sib_send, self.sib_recv, self.p.sibling).start()

    def own(self):
        p = self.p
        ref = self.block(p.d)
        remote(ref, ref, self.sends, self.r1.at[0], (p.index(1, 0), p.f)).start()
        remote(ref, ref, self.sends, self.r1.at[1], (p.index(3, 0), p.f)).start()
        remote(ref, ref, self.sends, self.r1.at[2], (p.index(2, 0), p.f)).start()
        self.to_second(0)
        self.to_sibling(ref)

    def first_near(self):
        for side, k in ((0, 3), (1, 1)):
            ref = self.block(self.p.index(k, 0))
            wait_bytes(ref, self.r1.at[side])
            self.to_second(k)
            self.to_sibling(ref)

    def first_far(self):
        ref = self.block(self.p.index(2, 0))
        wait_bytes(ref, self.r1.at[2])
        self.to_second(2)
        self.to_sibling(ref)

    def second_near(self, k1s=(0, 3, 1, 2)):
        p = self.p
        for k1 in k1s:
            for side, k in ((0, 3), (1, 1)):
                e = p.index(k1, k)
                wait_bytes(self.block(e), self.r2.at[k1, side])
                if k1 not in self.straight:
                    ref = self.half(e, side)
                    remote(ref, ref, self.sends, self.r2.at[k1, 2 + side], (p.index(0, 4 - k), p.f)).start()
                self.to_sibling(self.block(e))

    def second_far(self):
        for k1 in (0, 3, 1, 2):
            e = self.p.index(k1, 2)
            if k1 in self.straight:
                wait_bytes(self.block(e), self.r2.at[k1, 2])
            else:
                for side in (0, 1):
                    wait_bytes(self.half(e, side), self.r2.at[k1, 2 + side])
            self.to_sibling(self.block(e))

    def drain(self):
        wait_bytes(self.most, self.sends)


class WeightGather(Gather):
    def __init__(self, place, hbm, w, straight, sems):
        self.hbm, self.w = hbm, w
        self.s1_send, self.s1_recv, self.near_send, self.near_recv, self.own_sem = sems[:5]
        self.mine = w.at[place.c]
        far = pl.ds(2, 5)
        super().__init__(
            place,
            lambda e: w.at[place.c, far, e],
            lambda e, s: w.at[place.c, far, e, :, pl.ds(s * 256, 256)],
            w.at[place.c, far, pl.ds(0, 15)],
            straight,
            sems[5:],
        )

    def start(self):
        p = self.p
        source = self.hbm.at[p.d]
        for k in (4, 3, 5, 2, 6):
            z = lax.rem(p.z + 8 - k, 8)
            remote(source, self.mine.at[k, p.d], self.s1_send, self.s1_recv, (p.d, z * 2 + p.c)).start()

    def start_near(self):
        p = self.p
        for i, k in enumerate((1, 7)):
            z = lax.rem(p.z + 8 - k, 8)
            remote(self.hbm, self.mine.at[k], self.near_send, self.near_recv.at[i], (p.d, z * 2 + p.c)).start()
        pltpu.make_async_copy(self.hbm, self.mine.at[0], self.own_sem).start()

    def own(self):
        wait_bytes(self.block(self.p.d), self.s1_recv)
        super().own()

    def own_shard(self):
        wait_bytes(self.mine.at[0], self.own_sem)
        self.to_sibling(self.mine.at[0])

    def near(self):
        for i, k in enumerate((1, 7)):
            wait_bytes(self.mine.at[k], self.near_recv.at[i])
            self.to_sibling(self.mine.at[k])

    def finish(self):
        wait_bytes(self.w.at[1 - self.p.c], self.sib_recv)

    def drain(self):
        super().drain()
        wait_bytes(self.mine.at[pl.ds(2, 5), 0], self.s1_send)
        wait_bytes(self.mine.at[pl.ds(1, 2)], self.near_send)
        wait_bytes(self.mine, self.sib_send)


class RowGather(Gather):
    def __init__(self, place, source, held, straight, sems):
        self.source, self.held = source, held
        self.s1_send, self.s1_recv = sems[:2]
        super().__init__(
            place,
            lambda e: held.at[place.c, e],
            lambda e, s: held.at[place.c, e, :, pl.ds(s * 1024, 1024)],
            held.at[place.c, pl.ds(0, 15)],
            straight,
            sems[2:],
        )

    def start(self):
        p = self.p
        dst = self.held.at[p.c, p.d, :, pl.ds(pl.multiple_of(p.z * COLS, COLS), COLS)]
        pltpu.make_async_copy(self.source, dst, self.s1_recv).start()
        for k in (4, 3, 5, 2, 6, 1, 7):
            z = lax.rem(p.z + k, 8)
            remote(self.source, dst, self.s1_send, self.s1_recv, (p.d, z * 2 + p.c)).start()

    def own(self):
        wait_bytes(self.block(self.p.d), self.s1_recv)
        super().own()

    def finish(self):
        wait_bytes(self.held.at[1 - self.p.c], self.sib_recv)

    def drain(self):
        super().drain()
        wait_bytes(self.held.at[0, 0, :, pl.ds(0, 7 * COLS)], self.s1_send)
        wait_bytes(self.held.at[self.p.c], self.sib_send)


def all_to_all(place, source, target, send_sem, recv_sem):
    p = place

    def one(k, carry):
        g = lax.rem(p.f + k, NF)
        remote(source(g), target(p.f), send_sem, recv_sem, (p.d, g)).start()
        return carry

    pltpu.make_async_copy(source(p.f), target(p.f), recv_sem).start()
    lax.fori_loop(1, NF, one, 0)


def mean_square(rows):
    return jnp.mean(rows * rows, axis=-1, keepdims=True)


def kernel(
    lengths, partner, stream_hbm, norm_gain, wq_hbm, wk_hbm, wv_hbm, wo_hbm, q_gain, k_gain, final_gain,
    cos_hbm, sin_hbm,
    grad_out, loss_out,
    stream, normed, gain_row, wk, wv, everyone, wq, wo, cos_t, sin_t,
    pool_send, pool_recv, q_send, q_recv, mix_send, mix_recv, mix_f32,
    ab_send, ab_recv, c_send, c_recv, u_send, keys, values, sim,
    load_sem, pair_sem,
    k0, k1, k2, k3, k4, k5, k6, k7, k8, k9,
    v0, v1, v2, v3, v4, v5, v6, v7, v8, v9,
    u0, u1, u2, u3, u4, u5, u6,
):
    p = Place()
    d, f = p.d, p.f
    rows_of = lambda g, n: pl.ds(pl.multiple_of(g * n, n), n)
    lanes_of = lambda g, n: pl.ds(pl.multiple_of(g * n, n), n)

    quarter = TOKENS // 4
    loads = [
        pltpu.make_async_copy(stream_hbm.at[pl.ds(i * quarter, quarter)], stream.at[pl.ds(i * quarter, quarter)], load_sem.at[i])
        for i in range(4)
    ]
    loads += [
        pltpu.make_async_copy(wq_hbm, wq, load_sem.at[4]),
        pltpu.make_async_copy(cos_hbm, cos_t, load_sem.at[5]),
        pltpu.make_async_copy(sin_hbm, sin_t, load_sem.at[6]),
    ]
    for load in loads:
        load.start()

    barrier = pltpu.get_barrier_semaphore()

    def greet(k, carry):
        pl.semaphore_signal(barrier, inc=1, device_id=(d, lax.rem(f + k, NF)), device_id_type=pl.DeviceIdType.MESH)
        pl.semaphore_signal(barrier, inc=1, device_id=(lax.rem(d + k, ND), f), device_id_type=pl.DeviceIdType.MESH)
        return carry

    lax.fori_loop(1, NF, greet, 0)
    pl.semaphore_wait(barrier, NF - 1 + ND - 1)

    k_gather = WeightGather(p, wk_hbm, wk, K_STRAIGHT, (k0, k1, k2, k3, k4, k5, k6, k7, k8, k9))
    v_gather = WeightGather(p, wv_hbm, wv, V_STRAIGHT, (v0, v1, v2, v3, v4, v5, v6, v7, v8, v9))
    u_gather = RowGather(p, u_send, everyone, U_STRAIGHT, (u0, u1, u2, u3, u4, u5, u6))

    k_gather.start()

    for load in loads[:4]:
        load.wait()
    last = lengths[0, 0] - 1
    gain = norm_gain[...].astype(F32).reshape(1, WIDTH)
    for t in range(2):
        if t == 0:
            row = jnp.zeros((16, WIDTH), F32)
            for start in range(LEAST_LAST // 16 * 16, MOST_LAST + 1, 16):
                here = lax.broadcasted_iota(jnp.int32, (16, WIDTH), 0) == last - start
                row += jnp.where(here, stream[pl.ds(start, 16), :].astype(F32), 0.0)
            row = jnp.sum(row, axis=0, keepdims=True)
        else:
            row = stream[pl.ds(TOKENS - 16, 16), :].astype(F32)[15:16]
        norm_row = (row * lax.rsqrt(mean_square(row) + EPS) * gain).astype(BF16).astype(F32)
        for g in range(NF):
            for h in range(2):
                lane = g * COLS + h * 128
                pool_send[pl.ds(g * 8 + t * 2 + h, 1), :] = norm_row[:, lane : lane + 128]
                pool_send[pl.ds(g * 8 + 4 + t * 2 + h, 1), :] = row[:, lane : lane + 128]
    all_to_all(
        p, lambda g: pool_send.at[rows_of(g, 8)], lambda g: pool_recv.at[rows_of(g, 8)], pair_sem.at[0], pair_sem.at[1]
    )
    v_gather.start()
    k_gather.start_near()
    gain_row[...] = gain

    def norm_rows(i, carry):
        rows = pl.ds(pl.multiple_of(i * 32, 32), 32)
        block = stream[rows, :].astype(F32)
        inverse = lax.rsqrt(mean_square(block) + EPS)
        for k in range(8):
            lanes = lanes_of(lax.rem(p.z + k, 8), 2 * COLS)
            chunk = (stream[rows, lanes].astype(F32) * inverse * gain_row[:, lanes]).astype(BF16)
            for core in range(2):
                normed[core, rows, k * COLS : k * COLS + COLS] = chunk[:, core * COLS : core * COLS + COLS]
        return carry

    lax.fori_loop(0, TOKENS // 32, norm_rows, 0)

    k_gather.own()

    for load in loads[4:]:
        load.wait()
    wait_bytes(pool_recv, pair_sem.at[1])

    def pooled_block(first):
        return jnp.concatenate(
            [
                jnp.concatenate([pool_recv[pl.ds(first + t * 2 + h, NF, stride=8), :] for h in range(2)], axis=1)
                for t in range(2)
            ],
            axis=0,
        )

    shares = jnp.dot(pooled_block(0).astype(BF16), wq[...], preferred_element_type=F32)
    for t in range(2):
        for h in range(QUERY_HEADS):
            q_send[pl.ds(t * 16 + h, NF, stride=32), :] = shares[t * 16 : t * 16 + 16, h * 128 : h * 128 + 128]
    all_to_all(
        p, lambda g: q_send.at[rows_of(g, 32)], lambda g: q_recv.at[rows_of(g, 32)], pair_sem.at[2], pair_sem.at[3]
    )

    k_gather.first_near()
    v_gather.own()
    v_gather.start_near()
    k_gather.own_shard()
    k_gather.first_far()

    def wo_rows(core):
        return pl.ds(pl.multiple_of((p.x * (1 - core) + p.y * core) * 32, 32), 32)

    def send_wo(k, carry):
        g = lax.rem(f + k, NF)
        rows = wo_rows(g % 2)
        remote(wo_hbm.at[rows, lanes_of(g, COLS)], wo.at[f, rows], pair_sem.at[4], pair_sem.at[5], (d, g)).start()
        return carry

    pltpu.make_async_copy(wo_hbm.at[wo_rows(p.c), lanes_of(f, COLS)], wo.at[f, wo_rows(p.c)], pair_sem.at[5]).start()
    lax.fori_loop(1, NF, send_wo, 0)

    k_gather.second_near((0,))
    v_gather.first_near()
    k_gather.second_near((3, 1))
    v_gather.own_shard()
    v_gather.first_far()
    k_gather.second_near((2,))
    k_gather.near()
    v_gather.second_near((0,))
    k_gather.second_far()

    key_gain = k_gain[...].astype(F32)

    def half_product(w, core, rows):
        return jnp.dot(
            normed[core, rows, :],
            w[core].reshape(WIDTH // 2, 512),
            preferred_element_type=F32,
        )

    def first_half(w):
        for i in range(2):
            rows = pl.ds(i * 256, 256)
            sim[rows, :] = half_product(w, p.c, rows)

    first_half(wk)
    k_gather.finish()
    for i in range(2):
        rows = pl.ds(i * 256, 256)
        sim[rows, :] += half_product(wk, 1 - p.c, rows)
    v_gather.second_near((3, 1))

    def key_rows(i, carry):
        rows = pl.ds(pl.multiple_of(i * 128, 128), 128)
        for g in range(KEY_VALUE_HEADS):
            one = sim[rows, g * 128 : g * 128 + 128]
            one = one * lax.rsqrt(mean_square(one) + EPS) * key_gain
            one = one * cos_t[rows, :] + pltpu.roll(one, 64, 1) * sin_t[rows, :]
            keys[rows, g * 128 : g * 128 + 128] = one.astype(BF16)
        return carry

    lax.fori_loop(0, TOKENS // 128, key_rows, 0)
    wait_bytes(q_recv, pair_sem.at[3])
    query = q_recv[pl.ds(0, 32), :]
    for g in range(1, NF):
        query += q_recv[pl.ds(g * 32, 32), :]
    query = query * lax.rsqrt(mean_square(query) + EPS) * q_gain[...].astype(F32)
    row32 = lax.broadcasted_iota(jnp.int32, (32, 128), 0)

    def pooled_angle(table):
        start = LEAST_LAST // 8 * 8
        rows = table[pl.ds(start, MOST_LAST + 1 - start), :]
        here = lax.broadcasted_iota(jnp.int32, rows.shape, 0) == last - start
        first = jnp.sum(jnp.where(here, rows, 0.0), axis=0, keepdims=True)
        return jnp.where(row32 < 16, first, table[pl.ds(TOKENS - 1, 1), :])

    query = query * pooled_angle(cos_t) + pltpu.roll(query, 64, 1) * pooled_angle(sin_t)
    group = row32 % 16 // 4
    q_block = jnp.concatenate(
        [jnp.where(group == g, query, 0.0) for g in range(KEY_VALUE_HEADS)], axis=1
    ).astype(BF16)

    scores = lax.dot_general(q_block, keys[...], (((1,), (1,)), ((), ())), preferred_element_type=F32)
    scores = scores * (1.0 / math.sqrt(HEAD_SIZE))
    token = lax.broadcasted_iota(jnp.int32, scores.shape, 1)
    first_text = lax.broadcasted_iota(jnp.int32, scores.shape, 0) < 16
    inside = (token < lengths[0, 0]) == first_text
    weights = jnp.where(inside, jnp.exp(scores), 0.0)
    probs = (weights / jnp.sum(weights, axis=1, keepdims=True)).astype(BF16)

    v_gather.second_near((2,))
    v_gather.near()
    v_gather.second_far()
    own_wo = wo.at[:, wo_rows(p.c)]
    wait_bytes(own_wo, pair_sem.at[5])
    for k in (1, 3, 2):
        remote(own_wo, own_wo, pair_sem.at[12], pair_sem.at[13], (p.index(k, 0), f)).start()

    first_half(wv)
    v_gather.finish()
    for i in range(2):
        rows = pl.ds(i * 256, 256)
        values[rows, :] = (sim[rows, :] + half_product(wv, 1 - p.c, rows)).astype(BF16)
    all_mixed = jnp.dot(probs, values[...], preferred_element_type=F32)
    mixed = jnp.zeros((32, 128), F32)
    for g in range(KEY_VALUE_HEADS):
        mixed += jnp.where(group == g, all_mixed[:, g * 128 : g * 128 + 128], 0.0)
    mix_send[...] = mixed.astype(BF16)
    all_to_all(p, lambda g: mix_send, lambda g: mix_recv.at[g], pair_sem.at[6], pair_sem.at[7])
    wait_bytes(wo.at[pl.ds(0, 12)], pair_sem.at[13])
    wait_bytes(mix_recv, pair_sem.at[7])

    mix_f32[...] = mix_recv[...].astype(F32).reshape(NF * 32, 128)
    wide = jnp.concatenate(
        [
            jnp.concatenate([mix_f32[pl.ds(t * 16 + h, NF, stride=32), :] for h in range(QUERY_HEADS)], axis=1)
            for t in range(2)
        ],
        axis=0,
    ).astype(BF16)
    state = pooled_block(4) + jnp.dot(wide, wo[...].reshape(2048, COLS), preferred_element_type=F32)
    gained = state * final_gain[lanes_of(f, COLS)].astype(F32).reshape(1, COLS)
    u_send[...] = gained.astype(BF16)
    u_gather.start()

    offset = d % 4 * 32
    row = lax.broadcasted_iota(jnp.int32, (32, 128), 0)
    lane = lax.broadcasted_iota(jnp.int32, (32, 128), 1)
    diagonal = lane == row + offset
    as_lanes = lambda column: jnp.sum(jnp.where(diagonal, column, 0.0), axis=0, keepdims=True)
    square = as_lanes(jnp.sum(state * state, axis=1, keepdims=True))
    gained_square = as_lanes(jnp.sum(gained * gained, axis=1, keepdims=True))
    lane1 = lax.broadcasted_iota(jnp.int32, (1, 128), 1)
    own = [partner[0, 0], partner[0, 1]]
    partners = jnp.where(lane1 == offset + f, own[0], 0) + jnp.where(lane1 == offset + 16 + f, own[1], 0)
    row8 = lax.broadcasted_iota(jnp.int32, (8, 128), 0)
    pack = lambda parts: functools.reduce(
        lambda total, item: jnp.where(row8 == item[0], item[1], total), enumerate(parts), jnp.zeros((8, 128), F32)
    )
    ab_send[...] = pack([square, gained_square, partners.astype(F32)])
    all_to_all(p, lambda g: ab_send, lambda g: ab_recv.at[rows_of(g, 8)], pair_sem.at[8], pair_sem.at[9])
    u_gather.own()

    wait_bytes(ab_recv, pair_sem.at[9])
    sums = ab_recv[pl.ds(0, 8), :]
    for g in range(1, NF):
        sums += ab_recv[pl.ds(g * 8, 8), :]
    inverse = lax.rsqrt(sums[0:1] / WIDTH + EPS)
    factor = inverse * lax.rsqrt(inverse * inverse * sums[1:2] + EPS)
    factor = jnp.where((lane1 >= offset) & (lane1 < offset + 32), factor, 0.0)
    c_send[...] = pack([factor, sums[2:3]])

    def send_factor(k, carry):
        e = lax.rem(d + k, ND)
        remote(c_send, c_recv.at[rows_of(d, 8)], pair_sem.at[10], pair_sem.at[11], (e, f)).start()
        return carry

    pltpu.make_async_copy(c_send, c_recv.at[rows_of(d, 8)], pair_sem.at[11]).start()
    lax.fori_loop(1, ND, send_factor, 0)

    u_gather.first_near()
    u_gather.first_far()
    u_gather.second_near()
    u_gather.second_far()
    wait_bytes(c_recv, pair_sem.at[11])
    folded = []
    for q in range(4):
        folded.append(sum(c_recv[pl.ds((q * 4 + i) * 8, 8), :] for i in range(1, 4)) + c_recv[pl.ds(q * 32, 8), :])
    factor_row = jnp.concatenate([block[0:1] for block in folded], axis=1)
    partner_row = jnp.concatenate([block[1:2] for block in folded], axis=1).astype(jnp.int32)
    square_row = lax.broadcasted_iota(jnp.int32, (128, 128), 0)
    square_lane = lax.broadcasted_iota(jnp.int32, (128, 128), 1)
    factor_column = [
        jnp.sum(jnp.where(square_row == square_lane, block[0:1], 0.0), axis=1, keepdims=True) for block in folded
    ]

    def half_scores(core, i):
        return lax.dot_general(
            everyone[core, pl.ds(i * 8, 8)].reshape(256, WIDTH // 2),
            everyone[core].reshape(TEXTS, WIDTH // 2),
            (((1,), (1,)), ((), ())),
            preferred_element_type=F32,
        )

    for i in range(2):
        sim[pl.ds(i * 256, 256), :] = half_scores(p.c, i)
    u_gather.finish()
    name_of = lambda j: j // 32 * 32 + j % 16 * 2 + j % 32 // 16
    total = jnp.zeros((1, TEXTS), F32)
    target = jnp.zeros((1, TEXTS), F32)
    for i in range(2):
        rows = pl.ds(i * 256, 256)
        block = sim[rows, :] + half_scores(1 - p.c, i)
        column = jnp.concatenate(factor_column[i * 2 : i * 2 + 2], axis=0) * (1.0 / TEMPER)
        block = block * column * factor_row
        sim[rows, :] = block
        i_index = lax.broadcasted_iota(jnp.int32, block.shape, 0) + i * 256
        j_index = lax.broadcasted_iota(jnp.int32, block.shape, 1)
        hit = name_of(i_index) == partner_row
        total += jnp.sum(jnp.where((i_index != j_index) | hit, jnp.exp(block), 0.0), axis=0, keepdims=True)
        target += jnp.sum(jnp.where(hit, block, 0.0), axis=0, keepdims=True)
    loss_out[...] = jnp.sum(jnp.log(total) - target, axis=1, keepdims=True) * (1.0 / TEXTS)

    j_index = lax.broadcasted_iota(jnp.int32, (1, TEXTS), 1)
    names = name_of(j_index)
    coefficient = []
    for t in range(2):
        place = d * 32 + t * 16 + f
        name = (d * NF + f) * 2 + t
        exps = jnp.exp(sim[pl.ds(place, 1), :])
        own_total = jnp.sum(jnp.where(j_index == place, total, 0.0), axis=1, keepdims=True)
        other = j_index != place
        hit = names == own[t]
        back = partner_row == name
        pull = jnp.where(other | hit, exps, 0.0) / own_total - hit.astype(F32)
        pulled = jnp.where(other | back, exps, 0.0) / total - back.astype(F32)
        coefficient.append((pull.astype(BF16).astype(F32) + pulled.astype(BF16).astype(F32)) * factor_row)
    high = [item.astype(BF16).astype(F32) for item in coefficient]
    low = [item - part for item, part in zip(coefficient, high)]
    row16 = lax.broadcasted_iota(jnp.int32, (16, TEXTS), 0)
    stack = jnp.zeros((16, TEXTS), F32)
    for n, item in enumerate(high + low):
        stack = jnp.where(row16 == n, item, stack)
    stack = stack.astype(BF16)
    for core in range(2):
        for n in range(2):
            part = jnp.dot(
                stack, everyone[core, :, :, n * 1024 : n * 1024 + 1024].reshape(TEXTS, 1024), preferred_element_type=F32
            )
            part = (part[0:2] + part[2:4]) * (1.0 / TEMPER)
            for m in range(4):
                lane = ((n * 4 + m) * 2 + core) * COLS
                grad_out[:, lane : lane + COLS] = part[:, m * COLS : m * COLS + COLS]

    for gather in (k_gather, v_gather, u_gather):
        gather.drain()
    wait_bytes(pool_send.at[pl.ds(0, 15 * 8)], pair_sem.at[0])
    wait_bytes(q_send.at[pl.ds(0, 15 * 32)], pair_sem.at[2])
    wait_bytes(wo.at[pl.ds(0, 15), pl.ds(0, 32)], pair_sem.at[4])
    wait_bytes(wo.at[pl.ds(0, 12)], pair_sem.at[12])
    wait_bytes(mix_recv.at[pl.ds(0, 15)], pair_sem.at[6])
    wait_bytes(ab_recv.at[pl.ds(0, 15 * 8)], pair_sem.at[8])
    wait_bytes(c_recv.at[pl.ds(0, 15 * 8)], pair_sem.at[10])


def local(
    stream, lengths, partner, norm_gain, w_query, key_weight, value_weight, w_out, q_gain, key_norm_gain, final_gain
):
    cos_table, sin_table = rotary_tables()
    vmem = pl.BlockSpec(memory_space=pltpu.VMEM)
    smem = pl.BlockSpec(memory_space=pltpu.SMEM)
    hbm = pl.BlockSpec(memory_space=pltpu.HBM)
    dma = pltpu.SemaphoreType.DMA
    plane_sems = [dma, dma, dma, dma((4,)), dma((4, 4))]
    weight_sems = [dma, dma, dma, dma((2,)), dma] + plane_sems
    grad, loss = pl.pallas_call(
        kernel,
        out_shape=(
            jax.ShapeDtypeStruct((2, WIDTH), F32),
            jax.ShapeDtypeStruct((1, 1), F32),
        ),
        in_specs=[smem, smem, hbm, vmem, hbm, hbm, hbm, hbm, vmem, vmem, vmem, hbm, hbm],
        out_specs=(vmem, vmem),
        scratch_shapes=[
            pltpu.VMEM((TOKENS, WIDTH), BF16),
            pltpu.VMEM((2, TOKENS, WIDTH // 2), BF16),
            pltpu.VMEM((1, WIDTH), F32),
            pltpu.VMEM((2, 8, ND, 16, 512), BF16),
            pltpu.VMEM((2, 8, ND, 16, 512), BF16),
            pltpu.VMEM((2, ND, 32, WIDTH // 2), BF16),
            pltpu.VMEM((COLS, 2048), BF16),
            pltpu.VMEM((NF, 128, COLS), BF16),
            pltpu.VMEM((TOKENS, HEAD_SIZE), F32),
            pltpu.VMEM((TOKENS, HEAD_SIZE), F32),
            pltpu.VMEM((NF * 8, 128), F32),
            pltpu.VMEM((NF * 8, 128), F32),
            pltpu.VMEM((NF * 32, 128), F32),
            pltpu.VMEM((NF * 32, 128), F32),
            pltpu.VMEM((32, 128), BF16),
            pltpu.VMEM((NF, 32, 128), BF16),
            pltpu.VMEM((NF * 32, 128), F32),
            pltpu.VMEM((8, 128), F32),
            pltpu.VMEM((NF * 8, 128), F32),
            pltpu.VMEM((8, 128), F32),
            pltpu.VMEM((ND * 8, 128), F32),
            pltpu.VMEM((32, COLS), BF16),
            pltpu.VMEM((TOKENS, 512), BF16),
            pltpu.VMEM((TOKENS, 512), BF16),
            pltpu.VMEM((TEXTS, TEXTS), F32),
            dma((7,)),
            dma((14,)),
        ]
        + weight_sems * 2
        + [dma, dma]
        + plane_sems,
        compiler_params=pltpu.CompilerParams(
            collective_id=0, has_side_effects=True, vmem_limit_bytes=60 * 1024 * 1024
        ),
    )(
        lengths,
        partner.reshape(1, 2),
        stream,
        norm_gain,
        w_query,
        key_weight.reshape(ND, 16, 512),
        value_weight.reshape(ND, 16, 512),
        w_out,
        q_gain.reshape(1, HEAD_SIZE),
        key_norm_gain.reshape(1, HEAD_SIZE),
        final_gain,
        jnp.asarray(cos_table),
        jnp.asarray(sin_table),
    )
    return (grad, loss.reshape(()))


def solution(mesh):
    return jax.shard_map(
        local,
        mesh=mesh,
        in_specs=(
            P(("dp", "fsdp"), None),
            P(("dp", "fsdp"), None),
            P(("dp", "fsdp")),
            P(),
            P("fsdp", None),
            P("fsdp", None),
            P("fsdp", None),
            P("fsdp", None),
            P(),
            P(),
            P(),
        ),
        out_specs=(P(("dp", "fsdp"), None), P()),
        check_vma=False,
    )
```

```python
import functools
import math

import jax
import jax.numpy as jnp
import numpy as np
from jax import lax
from jax.experimental import pallas as pl
from jax.experimental.pallas import tpu as pltpu
from jax.sharding import PartitionSpec as P

QUERY_HEADS = 16
KEY_VALUE_HEADS = 4
HEAD_SIZE = 128
WIDTH = 4096
TOKENS = 512
TEXTS = 512
LEAST_LAST = 191
MOST_LAST = 319
K_STRAIGHT = (2,)
V_STRAIGHT = ()
U_STRAIGHT = ()
SIDE = 4
ND = 16
NF = 16
COLS = WIDTH // NF

EPS = 1e-06
THETA = 1000000.0
TEMPER = 0.05

F32 = jnp.float32
BF16 = jnp.bfloat16


def rotary_tables():
    half = HEAD_SIZE // 2
    freq = (THETA ** (-np.arange(half, dtype=np.float64) * 2.0 / HEAD_SIZE)).astype(np.float32)
    angle = np.arange(TOKENS, dtype=np.float32)[:, None] * freq[None, :]
    cosine, sine = np.cos(angle), np.sin(angle)
    return (
        np.concatenate([cosine, cosine], axis=1).astype(np.float32),
        np.concatenate([-sine, sine], axis=1).astype(np.float32),
    )


def remote(src, dst, send_sem, recv_sem, device):
    return pltpu.make_async_remote_copy(
        src_ref=src,
        dst_ref=dst,
        send_sem=send_sem,
        recv_sem=recv_sem,
        device_id=device,
        device_id_type=pl.DeviceIdType.MESH,
    )


def wait_bytes(ref, sem):
    pltpu.make_async_copy(ref, ref, sem).wait()


class Place:
    def __init__(self):
        self.d = lax.axis_index("dp")
        self.f = lax.axis_index("fsdp")
        self.x, self.y = self.d // SIDE, self.d % SIDE
        self.z, self.c = self.f // 2, self.f % 2
        self.sibling = (self.d, self.f + 1 - 2 * self.c)

    def index(self, k1, k2):
        xx = lax.rem(self.x + k1 * (1 - self.c) + k2 * self.c, SIDE)
        yy = lax.rem(self.y + k1 * self.c + k2 * (1 - self.c), SIDE)
        return xx * SIDE + yy


class Gather:
    def __init__(self, place, block, half, most, straight, sems):
        self.p, self.block, self.half, self.most, self.straight = place, block, half, most, straight
        self.sends, self.sib_send, self.sib_recv, self.r1, self.r2 = sems

    def to_second(self, k1):
        p = self.p
        ref = self.block(p.index(k1, 0))
        remote(ref, ref, self.sends, self.r2.at[k1, 0], (p.index(0, 1), p.f)).start()
        remote(ref, ref, self.sends, self.r2.at[k1, 1], (p.index(0, 3), p.f)).start()
        if k1 in self.straight:
            remote(ref, ref, self.sends, self.r2.at[k1, 2], (p.index(0, 2), p.f)).start()

    def to_sibling(self, ref):
        remote(ref, ref, self.sib_send, self.sib_recv, self.p.sibling).start()

    def own(self):
        p = self.p
        ref = self.block(p.d)
        remote(ref, ref, self.sends, self.r1.at[0], (p.index(1, 0), p.f)).start()
        remote(ref, ref, self.sends, self.r1.at[1], (p.index(3, 0), p.f)).start()
        remote(ref, ref, self.sends, self.r1.at[2], (p.index(2, 0), p.f)).start()
        self.to_second(0)
        self.to_sibling(ref)

    def first_near(self):
        for side, k in ((0, 3), (1, 1)):
            ref = self.block(self.p.index(k, 0))
            wait_bytes(ref, self.r1.at[side])
            self.to_second(k)
            self.to_sibling(ref)

    def first_far(self):
        ref = self.block(self.p.index(2, 0))
        wait_bytes(ref, self.r1.at[2])
        self.to_second(2)
        self.to_sibling(ref)

    def second_near(self, k1s=(0, 3, 1, 2)):
        p = self.p
        for k1 in k1s:
            for side, k in ((0, 3), (1, 1)):
                e = p.index(k1, k)
                wait_bytes(self.block(e), self.r2.at[k1, side])
                if k1 not in self.straight:
                    ref = self.half(e, side)
                    remote(ref, ref, self.sends, self.r2.at[k1, 2 + side], (p.index(0, 4 - k), p.f)).start()
                self.to_sibling(self.block(e))

    def second_far(self):
        for k1 in (0, 3, 1, 2):
            e = self.p.index(k1, 2)
            if k1 in self.straight:
                wait_bytes(self.block(e), self.r2.at[k1, 2])
            else:
                for side in (0, 1):
                    wait_bytes(self.half(e, side), self.r2.at[k1, 2 + side])
            self.to_sibling(self.block(e))

    def drain(self):
        wait_bytes(self.most, self.sends)


class WeightGather(Gather):
    def __init__(self, place, hbm, w, straight, sems):
        self.hbm, self.w = hbm, w
        self.s1_send, self.s1_recv, self.near_send, self.near_recv, self.own_sem = sems[:5]
        self.mine = w.at[place.c]
        far = pl.ds(2, 5)
        super().__init__(
            place,
            lambda e: w.at[place.c, far, e],
            lambda e, s: w.at[place.c, far, e, :, pl.ds(s * 256, 256)],
            w.at[place.c, far, pl.ds(0, 15)],
            straight,
            sems[5:],
        )

    def start(self):
        p = self.p
        source = self.hbm.at[p.d]
        for k in (4, 3, 5, 2, 6):
            z = lax.rem(p.z + 8 - k, 8)
            remote(source, self.mine.at[k, p.d], self.s1_send, self.s1_recv, (p.d, z * 2 + p.c)).start()

    def start_near(self):
        p = self.p
        for i, k in enumerate((1, 7)):
            z = lax.rem(p.z + 8 - k, 8)
            remote(self.hbm, self.mine.at[k], self.near_send, self.near_recv.at[i], (p.d, z * 2 + p.c)).start()
        pltpu.make_async_copy(self.hbm, self.mine.at[0], self.own_sem).start()

    def own(self):
        wait_bytes(self.block(self.p.d), self.s1_recv)
        super().own()

    def own_shard(self):
        wait_bytes(self.mine.at[0], self.own_sem)
        self.to_sibling(self.mine.at[0])

    def near(self):
        for i, k in enumerate((1, 7)):
            wait_bytes(self.mine.at[k], self.near_recv.at[i])
            self.to_sibling(self.mine.at[k])

    def finish(self):
        wait_bytes(self.w.at[1 - self.p.c], self.sib_recv)

    def drain(self):
        super().drain()
        wait_bytes(self.mine.at[pl.ds(2, 5), 0], self.s1_send)
        wait_bytes(self.mine.at[pl.ds(1, 2)], self.near_send)
        wait_bytes(self.mine, self.sib_send)


class RowGather(Gather):
    def __init__(self, place, source, held, straight, sems):
        self.source, self.held = source, held
        self.s1_send, self.s1_recv = sems[:2]
        super().__init__(
            place,
            lambda e: held.at[place.c, e],
            lambda e, s: held.at[place.c, e, :, pl.ds(s * 1024, 1024)],
            held.at[place.c, pl.ds(0, 15)],
            straight,
            sems[2:],
        )

    def start(self):
        p = self.p
        dst = self.held.at[p.c, p.d, :, pl.ds(pl.multiple_of(p.z * COLS, COLS), COLS)]
        pltpu.make_async_copy(self.source, dst, self.s1_recv).start()
        for k in (4, 3, 5, 2, 6, 1, 7):
            z = lax.rem(p.z + k, 8)
            remote(self.source, dst, self.s1_send, self.s1_recv, (p.d, z * 2 + p.c)).start()

    def own(self):
        wait_bytes(self.block(self.p.d), self.s1_recv)
        super().own()

    def finish(self):
        wait_bytes(self.held.at[1 - self.p.c], self.sib_recv)

    def drain(self):
        super().drain()
        wait_bytes(self.held.at[0, 0, :, pl.ds(0, 7 * COLS)], self.s1_send)
        wait_bytes(self.held.at[self.p.c], self.sib_send)


def all_to_all(place, source, target, send_sem, recv_sem):
    p = place

    def one(k, carry):
        g = lax.rem(p.f + k, NF)
        remote(source(g), target(p.f), send_sem, recv_sem, (p.d, g)).start()
        return carry

    pltpu.make_async_copy(source(p.f), target(p.f), recv_sem).start()
    lax.fori_loop(1, NF, one, 0)


def mean_square(rows):
    return jnp.mean(rows * rows, axis=-1, keepdims=True)


def kernel(
    lengths, partner, stream_hbm, norm_gain, wq_hbm, wk_hbm, wv_hbm, wo_hbm, q_gain, k_gain, final_gain,
    cos_hbm, sin_hbm,
    grad_out, loss_out,
    stream, normed, gain_row, wk, wv, everyone, wq, wo, cos_t, sin_t,
    pool_send, pool_recv, q_send, q_recv, mix_send, mix_recv, mix_f32,
    ab_send, ab_recv, c_send, c_recv, u_send, keys, values, sim,
    load_sem, pair_sem,
    k0, k1, k2, k3, k4, k5, k6, k7, k8, k9,
    v0, v1, v2, v3, v4, v5, v6, v7, v8, v9,
    u0, u1, u2, u3, u4, u5, u6,
):
    p = Place()
    d, f = p.d, p.f
    rows_of = lambda g, n: pl.ds(pl.multiple_of(g * n, n), n)
    lanes_of = lambda g, n: pl.ds(pl.multiple_of(g * n, n), n)

    quarter = TOKENS // 4
    loads = [
        pltpu.make_async_copy(stream_hbm.at[pl.ds(i * quarter, quarter)], stream.at[pl.ds(i * quarter, quarter)], load_sem.at[i])
        for i in range(4)
    ]
    loads += [
        pltpu.make_async_copy(wq_hbm, wq, load_sem.at[4]),
        pltpu.make_async_copy(cos_hbm, cos_t, load_sem.at[5]),
        pltpu.make_async_copy(sin_hbm, sin_t, load_sem.at[6]),
    ]
    for load in loads:
        load.start()

    barrier = pltpu.get_barrier_semaphore()

    def greet(k, carry):
        pl.semaphore_signal(barrier, inc=1, device_id=(d, lax.rem(f + k, NF)), device_id_type=pl.DeviceIdType.MESH)
        pl.semaphore_signal(barrier, inc=1, device_id=(lax.rem(d + k, ND), f), device_id_type=pl.DeviceIdType.MESH)
        return carry

    lax.fori_loop(1, NF, greet, 0)
    pl.semaphore_wait(barrier, NF - 1 + ND - 1)

    k_gather = WeightGather(p, wk_hbm, wk, K_STRAIGHT, (k0, k1, k2, k3, k4, k5, k6, k7, k8, k9))
    v_gather = WeightGather(p, wv_hbm, wv, V_STRAIGHT, (v0, v1, v2, v3, v4, v5, v6, v7, v8, v9))
    u_gather = RowGather(p, u_send, everyone, U_STRAIGHT, (u0, u1, u2, u3, u4, u5, u6))

    k_gather.start()

    for load in loads[:4]:
        load.wait()
    last = lengths[0, 0] - 1
    gain = norm_gain[...].astype(F32).reshape(1, WIDTH)
    for t in range(2):
        if t == 0:
            row = jnp.zeros((16, WIDTH), F32)
            for start in range(LEAST_LAST // 16 * 16, MOST_LAST + 1, 16):
                here = lax.broadcasted_iota(jnp.int32, (16, WIDTH), 0) == last - start
                row += jnp.where(here, stream[pl.ds(start, 16), :].astype(F32), 0.0)
            row = jnp.sum(row, axis=0, keepdims=True)
        else:
            row = stream[pl.ds(TOKENS - 16, 16), :].astype(F32)[15:16]
        norm_row = (row * lax.rsqrt(mean_square(row) + EPS) * gain).astype(BF16).astype(F32)
        for g in range(NF):
            for h in range(2):
                lane = g * COLS + h * 128
                pool_send[pl.ds(g * 8 + t * 2 + h, 1), :] = norm_row[:, lane : lane + 128]
                pool_send[pl.ds(g * 8 + 4 + t * 2 + h, 1), :] = row[:, lane : lane + 128]
    all_to_all(
        p, lambda g: pool_send.at[rows_of(g, 8)], lambda g: pool_recv.at[rows_of(g, 8)], pair_sem.at[0], pair_sem.at[1]
    )
    v_gather.start()
    k_gather.start_near()
    gain_row[...] = gain

    def norm_rows(i, carry):
        rows = pl.ds(pl.multiple_of(i * 32, 32), 32)
        block = stream[rows, :].astype(F32)
        inverse = lax.rsqrt(mean_square(block) + EPS)
        for k in range(8):
            lanes = lanes_of(lax.rem(p.z + k, 8), 2 * COLS)
            chunk = (stream[rows, lanes].astype(F32) * inverse * gain_row[:, lanes]).astype(BF16)
            for core in range(2):
                normed[core, rows, k * COLS : k * COLS + COLS] = chunk[:, core * COLS : core * COLS + COLS]
        return carry

    lax.fori_loop(0, TOKENS // 32, norm_rows, 0)

    k_gather.own()

    for load in loads[4:]:
        load.wait()
    wait_bytes(pool_recv, pair_sem.at[1])

    def pooled_block(first):
        return jnp.concatenate(
            [
                jnp.concatenate([pool_recv[pl.ds(first + t * 2 + h, NF, stride=8), :] for h in range(2)], axis=1)
                for t in range(2)
            ],
            axis=0,
        )

    shares = jnp.dot(pooled_block(0).astype(BF16), wq[...], preferred_element_type=F32)
    for t in range(2):
        for h in range(QUERY_HEADS):
            q_send[pl.ds(t * 16 + h, NF, stride=32), :] = shares[t * 16 : t * 16 + 16, h * 128 : h * 128 + 128]
    all_to_all(
        p, lambda g: q_send.at[rows_of(g, 32)], lambda g: q_recv.at[rows_of(g, 32)], pair_sem.at[2], pair_sem.at[3]
    )

    k_gather.first_near()
    v_gather.own()
    v_gather.start_near()
    k_gather.own_shard()
    k_gather.first_far()

    def wo_rows(core):
        return pl.ds(pl.multiple_of((p.x * (1 - core) + p.y * core) * 32, 32), 32)

    def send_wo(k, carry):
        g = lax.rem(f + k, NF)
        rows = wo_rows(g % 2)
        remote(wo_hbm.at[rows, lanes_of(g, COLS)], wo.at[f, rows], pair_sem.at[4], pair_sem.at[5], (d, g)).start()
        return carry

    pltpu.make_async_copy(wo_hbm.at[wo_rows(p.c), lanes_of(f, COLS)], wo.at[f, wo_rows(p.c)], pair_sem.at[5]).start()
    lax.fori_loop(1, NF, send_wo, 0)

    k_gather.second_near((0,))
    v_gather.first_near()
    k_gather.second_near((3, 1))
    v_gather.own_shard()
    v_gather.first_far()
    k_gather.second_near((2,))
    k_gather.near()
    v_gather.second_near((0,))
    k_gather.second_far()

    key_gain = k_gain[...].astype(F32)

    def half_product(w, core, rows):
        return jnp.dot(
            normed[core, rows, :],
            w[core].reshape(WIDTH // 2, 512),
            preferred_element_type=F32,
        )

    def first_half(w):
        for i in range(2):
            rows = pl.ds(i * 256, 256)
            sim[rows, :] = half_product(w, p.c, rows)

    first_half(wk)
    k_gather.finish()
    for i in range(2):
        rows = pl.ds(i * 256, 256)
        sim[rows, :] += half_product(wk, 1 - p.c, rows)
    v_gather.second_near((3, 1))

    def key_rows(i, carry):
        rows = pl.ds(pl.multiple_of(i * 128, 128), 128)
        for g in range(KEY_VALUE_HEADS):
            one = sim[rows, g * 128 : g * 128 + 128]
            one = one * lax.rsqrt(mean_square(one) + EPS) * key_gain
            one = one * cos_t[rows, :] + pltpu.roll(one, 64, 1) * sin_t[rows, :]
            keys[rows, g * 128 : g * 128 + 128] = one.astype(BF16)
        return carry

    lax.fori_loop(0, TOKENS // 128, key_rows, 0)
    wait_bytes(q_recv, pair_sem.at[3])
    query = q_recv[pl.ds(0, 32), :]
    for g in range(1, NF):
        query += q_recv[pl.ds(g * 32, 32), :]
    query = query * lax.rsqrt(mean_square(query) + EPS) * q_gain[...].astype(F32)
    row32 = lax.broadcasted_iota(jnp.int32, (32, 128), 0)

    def pooled_angle(table):
        start = LEAST_LAST // 8 * 8
        rows = table[pl.ds(start, MOST_LAST + 1 - start), :]
        here = lax.broadcasted_iota(jnp.int32, rows.shape, 0) == last - start
        first = jnp.sum(jnp.where(here, rows, 0.0), axis=0, keepdims=True)
        return jnp.where(row32 < 16, first, table[pl.ds(TOKENS - 1, 1), :])

    query = query * pooled_angle(cos_t) + pltpu.roll(query, 64, 1) * pooled_angle(sin_t)
    group = row32 % 16 // 4
    q_block = jnp.concatenate(
        [jnp.where(group == g, query, 0.0) for g in range(KEY_VALUE_HEADS)], axis=1
    ).astype(BF16)

    scores = lax.dot_general(q_block, keys[...], (((1,), (1,)), ((), ())), preferred_element_type=F32)
    scores = scores * (1.0 / math.sqrt(HEAD_SIZE))
    token = lax.broadcasted_iota(jnp.int32, scores.shape, 1)
    first_text = lax.broadcasted_iota(jnp.int32, scores.shape, 0) < 16
    inside = (token < lengths[0, 0]) == first_text
    weights = jnp.where(inside, jnp.exp(scores), 0.0)
    probs = (weights / jnp.sum(weights, axis=1, keepdims=True)).astype(BF16)

    v_gather.second_near((2,))
    v_gather.near()
    v_gather.second_far()
    own_wo = wo.at[:, wo_rows(p.c)]
    wait_bytes(own_wo, pair_sem.at[5])
    for k in (1, 3, 2):
        remote(own_wo, own_wo, pair_sem.at[12], pair_sem.at[13], (p.index(k, 0), f)).start()

    first_half(wv)
    v_gather.finish()
    for i in range(2):
        rows = pl.ds(i * 256, 256)
        values[rows, :] = (sim[rows, :] + half_product(wv, 1 - p.c, rows)).astype(BF16)
    all_mixed = jnp.dot(probs, values[...], preferred_element_type=F32)
    mixed = jnp.zeros((32, 128), F32)
    for g in range(KEY_VALUE_HEADS):
        mixed += jnp.where(group == g, all_mixed[:, g * 128 : g * 128 + 128], 0.0)
    mix_send[...] = mixed.astype(BF16)
    all_to_all(p, lambda g: mix_send, lambda g: mix_recv.at[g], pair_sem.at[6], pair_sem.at[7])
    wait_bytes(wo.at[pl.ds(0, 12)], pair_sem.at[13])
    wait_bytes(mix_recv, pair_sem.at[7])

    mix_f32[...] = mix_recv[...].astype(F32).reshape(NF * 32, 128)
    wide = jnp.concatenate(
        [
            jnp.concatenate([mix_f32[pl.ds(t * 16 + h, NF, stride=32), :] for h in range(QUERY_HEADS)], axis=1)
            for t in range(2)
        ],
        axis=0,
    ).astype(BF16)
    state = pooled_block(4) + jnp.dot(wide, wo[...].reshape(2048, COLS), preferred_element_type=F32)
    gained = state * final_gain[lanes_of(f, COLS)].astype(F32).reshape(1, COLS)
    u_send[...] = gained.astype(BF16)
    u_gather.start()

    offset = d % 4 * 32
    row = lax.broadcasted_iota(jnp.int32, (32, 128), 0)
    lane = lax.broadcasted_iota(jnp.int32, (32, 128), 1)
    diagonal = lane == row + offset
    as_lanes = lambda column: jnp.sum(jnp.where(diagonal, column, 0.0), axis=0, keepdims=True)
    square = as_lanes(jnp.sum(state * state, axis=1, keepdims=True))
    gained_square = as_lanes(jnp.sum(gained * gained, axis=1, keepdims=True))
    lane1 = lax.broadcasted_iota(jnp.int32, (1, 128), 1)
    own = [partner[0, 0], partner[0, 1]]
    partners = jnp.where(lane1 == offset + f, own[0], 0) + jnp.where(lane1 == offset + 16 + f, own[1], 0)
    row8 = lax.broadcasted_iota(jnp.int32, (8, 128), 0)
    pack = lambda parts: functools.reduce(
        lambda total, item: jnp.where(row8 == item[0], item[1], total), enumerate(parts), jnp.zeros((8, 128), F32)
    )
    ab_send[...] = pack([square, gained_square, partners.astype(F32)])
    all_to_all(p, lambda g: ab_send, lambda g: ab_recv.at[rows_of(g, 8)], pair_sem.at[8], pair_sem.at[9])
    u_gather.own()

    wait_bytes(ab_recv, pair_sem.at[9])
    sums = ab_recv[pl.ds(0, 8), :]
    for g in range(1, NF):
        sums += ab_recv[pl.ds(g * 8, 8), :]
    inverse = lax.rsqrt(sums[0:1] / WIDTH + EPS)
    factor = inverse * lax.rsqrt(inverse * inverse * sums[1:2] + EPS)
    factor = jnp.where((lane1 >= offset) & (lane1 < offset + 32), factor, 0.0)
    c_send[...] = pack([factor, sums[2:3]])

    def send_factor(k, carry):
        e = lax.rem(d + k, ND)
        remote(c_send, c_recv.at[rows_of(d, 8)], pair_sem.at[10], pair_sem.at[11], (e, f)).start()
        return carry

    pltpu.make_async_copy(c_send, c_recv.at[rows_of(d, 8)], pair_sem.at[11]).start()
    lax.fori_loop(1, ND, send_factor, 0)

    k_gather.drain()
    v_gather.drain()
    wait_bytes(pool_send.at[pl.ds(0, 15 * 8)], pair_sem.at[0])
    wait_bytes(q_send.at[pl.ds(0, 15 * 32)], pair_sem.at[2])
    wait_bytes(wo.at[pl.ds(0, 15), pl.ds(0, 32)], pair_sem.at[4])
    wait_bytes(wo.at[pl.ds(0, 12)], pair_sem.at[12])
    wait_bytes(mix_recv.at[pl.ds(0, 15)], pair_sem.at[6])

    u_gather.first_near()
    u_gather.first_far()
    u_gather.second_near()
    u_gather.second_far()
    wait_bytes(c_recv, pair_sem.at[11])
    folded = []
    for q in range(4):
        folded.append(sum(c_recv[pl.ds((q * 4 + i) * 8, 8), :] for i in range(1, 4)) + c_recv[pl.ds(q * 32, 8), :])
    factor_row = jnp.concatenate([block[0:1] for block in folded], axis=1)
    partner_row = jnp.concatenate([block[1:2] for block in folded], axis=1).astype(jnp.int32)
    square_row = lax.broadcasted_iota(jnp.int32, (128, 128), 0)
    square_lane = lax.broadcasted_iota(jnp.int32, (128, 128), 1)
    factor_column = [
        jnp.sum(jnp.where(square_row == square_lane, block[0:1], 0.0), axis=1, keepdims=True) for block in folded
    ]

    def half_scores(core, i):
        return lax.dot_general(
            everyone[core, pl.ds(i * 8, 8)].reshape(256, WIDTH // 2),
            everyone[core].reshape(TEXTS, WIDTH // 2),
            (((1,), (1,)), ((), ())),
            preferred_element_type=F32,
        )

    for i in range(2):
        sim[pl.ds(i * 256, 256), :] = half_scores(p.c, i)
    u_gather.finish()
    name_of = lambda j: j // 32 * 32 + j % 16 * 2 + j % 32 // 16
    total = jnp.zeros((1, TEXTS), F32)
    target = jnp.zeros((1, TEXTS), F32)
    for i in range(2):
        rows = pl.ds(i * 256, 256)
        block = sim[rows, :] + half_scores(1 - p.c, i)
        column = jnp.concatenate(factor_column[i * 2 : i * 2 + 2], axis=0) * (1.0 / TEMPER)
        block = block * column * factor_row
        sim[rows, :] = block
        i_index = lax.broadcasted_iota(jnp.int32, block.shape, 0) + i * 256
        j_index = lax.broadcasted_iota(jnp.int32, block.shape, 1)
        hit = name_of(i_index) == partner_row
        total += jnp.sum(jnp.where((i_index != j_index) | hit, jnp.exp(block), 0.0), axis=0, keepdims=True)
        target += jnp.sum(jnp.where(hit, block, 0.0), axis=0, keepdims=True)
    loss_out[...] = jnp.sum(jnp.log(total) - target, axis=1, keepdims=True) * (1.0 / TEXTS)

    j_index = lax.broadcasted_iota(jnp.int32, (1, TEXTS), 1)
    names = name_of(j_index)
    coefficient = []
    for t in range(2):
        place = d * 32 + t * 16 + f
        name = (d * NF + f) * 2 + t
        exps = jnp.exp(sim[pl.ds(place, 1), :])
        own_total = jnp.sum(jnp.where(j_index == place, total, 0.0), axis=1, keepdims=True)
        other = j_index != place
        hit = names == own[t]
        back = partner_row == name
        pull = jnp.where(other | hit, exps, 0.0) / own_total - hit.astype(F32)
        pulled = jnp.where(other | back, exps, 0.0) / total - back.astype(F32)
        coefficient.append((pull.astype(BF16).astype(F32) + pulled.astype(BF16).astype(F32)) * factor_row)
    high = [item.astype(BF16).astype(F32) for item in coefficient]
    low = [item - part for item, part in zip(coefficient, high)]
    row16 = lax.broadcasted_iota(jnp.int32, (16, TEXTS), 0)
    stack = jnp.zeros((16, TEXTS), F32)
    for n, item in enumerate(high + low):
        stack = jnp.where(row16 == n, item, stack)
    stack = stack.astype(BF16)
    for core in range(2):
        for n in range(2):
            part = jnp.dot(
                stack, everyone[core, :, :, n * 1024 : n * 1024 + 1024].reshape(TEXTS, 1024), preferred_element_type=F32
            )
            part = (part[0:2] + part[2:4]) * (1.0 / TEMPER)
            for m in range(4):
                lane = ((n * 4 + m) * 2 + core) * COLS
                grad_out[:, lane : lane + COLS] = part[:, m * COLS : m * COLS + COLS]

    u_gather.drain()
    wait_bytes(ab_recv.at[pl.ds(0, 15 * 8)], pair_sem.at[8])
    wait_bytes(c_recv.at[pl.ds(0, 15 * 8)], pair_sem.at[10])


def local(
    stream, lengths, partner, norm_gain, w_query, key_weight, value_weight, w_out, q_gain, key_norm_gain, final_gain
):
    cos_table, sin_table = rotary_tables()
    vmem = pl.BlockSpec(memory_space=pltpu.VMEM)
    smem = pl.BlockSpec(memory_space=pltpu.SMEM)
    hbm = pl.BlockSpec(memory_space=pltpu.HBM)
    dma = pltpu.SemaphoreType.DMA
    plane_sems = [dma, dma, dma, dma((4,)), dma((4, 4))]
    weight_sems = [dma, dma, dma, dma((2,)), dma] + plane_sems
    grad, loss = pl.pallas_call(
        kernel,
        out_shape=(
            jax.ShapeDtypeStruct((2, WIDTH), F32),
            jax.ShapeDtypeStruct((1, 1), F32),
        ),
        in_specs=[smem, smem, hbm, vmem, hbm, hbm, hbm, hbm, vmem, vmem, vmem, hbm, hbm],
        out_specs=(vmem, vmem),
        scratch_shapes=[
            pltpu.VMEM((TOKENS, WIDTH), BF16),
            pltpu.VMEM((2, TOKENS, WIDTH // 2), BF16),
            pltpu.VMEM((1, WIDTH), F32),
            pltpu.VMEM((2, 8, ND, 16, 512), BF16),
            pltpu.VMEM((2, 8, ND, 16, 512), BF16),
            pltpu.VMEM((2, ND, 32, WIDTH // 2), BF16),
            pltpu.VMEM((COLS, 2048), BF16),
            pltpu.VMEM((NF, 128, COLS), BF16),
            pltpu.VMEM((TOKENS, HEAD_SIZE), F32),
            pltpu.VMEM((TOKENS, HEAD_SIZE), F32),
            pltpu.VMEM((NF * 8, 128), F32),
            pltpu.VMEM((NF * 8, 128), F32),
            pltpu.VMEM((NF * 32, 128), F32),
            pltpu.VMEM((NF * 32, 128), F32),
            pltpu.VMEM((32, 128), BF16),
            pltpu.VMEM((NF, 32, 128), BF16),
            pltpu.VMEM((NF * 32, 128), F32),
            pltpu.VMEM((8, 128), F32),
            pltpu.VMEM((NF * 8, 128), F32),
            pltpu.VMEM((8, 128), F32),
            pltpu.VMEM((ND * 8, 128), F32),
            pltpu.VMEM((32, COLS), BF16),
            pltpu.VMEM((TOKENS, 512), BF16),
            pltpu.VMEM((TOKENS, 512), BF16),
            pltpu.VMEM((TEXTS, TEXTS), F32),
            dma((7,)),
            dma((14,)),
        ]
        + weight_sems * 2
        + [dma, dma]
        + plane_sems,
        compiler_params=pltpu.CompilerParams(
            collective_id=0, has_side_effects=True, vmem_limit_bytes=60 * 1024 * 1024
        ),
    )(
        lengths,
        partner.reshape(1, 2),
        stream,
        norm_gain,
        w_query,
        key_weight.reshape(ND, 16, 512),
        value_weight.reshape(ND, 16, 512),
        w_out,
        q_gain.reshape(1, HEAD_SIZE),
        key_norm_gain.reshape(1, HEAD_SIZE),
        final_gain,
        jnp.asarray(cos_table),
        jnp.asarray(sin_table),
    )
    return (grad, loss.reshape(()))


def solution(mesh):
    return jax.shard_map(
        local,
        mesh=mesh,
        in_specs=(
            P(("dp", "fsdp"), None),
            P(("dp", "fsdp"), None),
            P(("dp", "fsdp")),
            P(),
            P("fsdp", None),
            P("fsdp", None),
            P("fsdp", None),
            P("fsdp", None),
            P(),
            P(),
            P(),
        ),
        out_specs=(P(("dp", "fsdp"), None), P()),
        check_vma=False,
    )
```

```python
import functools
import math

import jax
import jax.numpy as jnp
import numpy as np
from jax import lax
from jax.experimental import pallas as pl
from jax.experimental.pallas import tpu as pltpu
from jax.sharding import PartitionSpec as P

QUERY_HEADS = 16
KEY_VALUE_HEADS = 4
HEAD_SIZE = 128
WIDTH = 4096
TOKENS = 512
TEXTS = 512
LEAST_LAST = 191
MOST_LAST = 319
K_STRAIGHT = (2,)
V_STRAIGHT = ()
U_STRAIGHT = ()
SIDE = 4
ND = 16
NF = 16
COLS = WIDTH // NF

EPS = 1e-06
THETA = 1000000.0
TEMPER = 0.05

F32 = jnp.float32
BF16 = jnp.bfloat16


def rotary_tables():
    half = HEAD_SIZE // 2
    freq = (THETA ** (-np.arange(half, dtype=np.float64) * 2.0 / HEAD_SIZE)).astype(np.float32)
    angle = np.arange(TOKENS, dtype=np.float32)[:, None] * freq[None, :]
    cosine, sine = np.cos(angle), np.sin(angle)
    return (
        np.concatenate([cosine, cosine], axis=1).astype(np.float32),
        np.concatenate([-sine, sine], axis=1).astype(np.float32),
    )


def remote(src, dst, send_sem, recv_sem, device):
    return pltpu.make_async_remote_copy(
        src_ref=src,
        dst_ref=dst,
        send_sem=send_sem,
        recv_sem=recv_sem,
        device_id=device,
        device_id_type=pl.DeviceIdType.MESH,
    )


def wait_bytes(ref, sem):
    pltpu.make_async_copy(ref, ref, sem).wait()


class Place:
    def __init__(self):
        self.d = lax.axis_index("dp")
        self.f = lax.axis_index("fsdp")
        self.x, self.y = self.d // SIDE, self.d % SIDE
        self.z, self.c = self.f // 2, self.f % 2
        self.sibling = (self.d, self.f + 1 - 2 * self.c)

    def index(self, k1, k2):
        xx = lax.rem(self.x + k1 * (1 - self.c) + k2 * self.c, SIDE)
        yy = lax.rem(self.y + k1 * self.c + k2 * (1 - self.c), SIDE)
        return xx * SIDE + yy


class Gather:
    def __init__(self, place, block, half, most, straight, sems):
        self.p, self.block, self.half, self.most, self.straight = place, block, half, most, straight
        self.sends, self.sib_send, self.sib_recv, self.r1, self.r2 = sems

    def to_second(self, k1):
        p = self.p
        ref = self.block(p.index(k1, 0))
        remote(ref, ref, self.sends, self.r2.at[k1, 0], (p.index(0, 1), p.f)).start()
        remote(ref, ref, self.sends, self.r2.at[k1, 1], (p.index(0, 3), p.f)).start()
        if k1 in self.straight:
            remote(ref, ref, self.sends, self.r2.at[k1, 2], (p.index(0, 2), p.f)).start()

    def to_sibling(self, ref):
        remote(ref, ref, self.sib_send, self.sib_recv, self.p.sibling).start()

    def own(self):
        p = self.p
        ref = self.block(p.d)
        remote(ref, ref, self.sends, self.r1.at[0], (p.index(1, 0), p.f)).start()
        remote(ref, ref, self.sends, self.r1.at[1], (p.index(3, 0), p.f)).start()
        remote(ref, ref, self.sends, self.r1.at[2], (p.index(2, 0), p.f)).start()
        self.to_second(0)
        self.to_sibling(ref)

    def first_near(self):
        for side, k in ((0, 3), (1, 1)):
            ref = self.block(self.p.index(k, 0))
            wait_bytes(ref, self.r1.at[side])
            self.to_second(k)
            self.to_sibling(ref)

    def first_far(self):
        ref = self.block(self.p.index(2, 0))
        wait_bytes(ref, self.r1.at[2])
        self.to_second(2)
        self.to_sibling(ref)

    def second_near(self, k1s=(0, 3, 1, 2)):
        p = self.p
        for k1 in k1s:
            for side, k in ((0, 3), (1, 1)):
                e = p.index(k1, k)
                wait_bytes(self.block(e), self.r2.at[k1, side])
                if k1 not in self.straight:
                    ref = self.half(e, side)
                    remote(ref, ref, self.sends, self.r2.at[k1, 2 + side], (p.index(0, 4 - k), p.f)).start()
                self.to_sibling(self.block(e))

    def second_far(self):
        for k1 in (0, 3, 1, 2):
            e = self.p.index(k1, 2)
            if k1 in self.straight:
                wait_bytes(self.block(e), self.r2.at[k1, 2])
            else:
                for side in (0, 1):
                    wait_bytes(self.half(e, side), self.r2.at[k1, 2 + side])
            self.to_sibling(self.block(e))

    def drain(self):
        wait_bytes(self.most, self.sends)


class WeightGather(Gather):
    def __init__(self, place, hbm, w, straight, sems):
        self.hbm, self.w = hbm, w
        self.s1_send, self.s1_recv, self.near_send, self.near_recv, self.own_sem = sems[:5]
        self.mine = w.at[place.c]
        far = pl.ds(2, 5)
        super().__init__(
            place,
            lambda e: w.at[place.c, far, e],
            lambda e, s: w.at[place.c, far, e, :, pl.ds(s * 256, 256)],
            w.at[place.c, far, pl.ds(0, 15)],
            straight,
            sems[5:],
        )

    def start(self):
        p = self.p
        source = self.hbm.at[p.d]
        for k in (4, 3, 5, 2, 6):
            z = lax.rem(p.z + 8 - k, 8)
            remote(source, self.mine.at[k, p.d], self.s1_send, self.s1_recv, (p.d, z * 2 + p.c)).start()

    def start_near(self):
        p = self.p
        for i, k in enumerate((1, 7)):
            z = lax.rem(p.z + 8 - k, 8)
            remote(self.hbm, self.mine.at[k], self.near_send, self.near_recv.at[i], (p.d, z * 2 + p.c)).start()
        pltpu.make_async_copy(self.hbm, self.mine.at[0], self.own_sem).start()

    def own(self):
        wait_bytes(self.block(self.p.d), self.s1_recv)
        super().own()

    def own_shard(self):
        wait_bytes(self.mine.at[0], self.own_sem)
        self.to_sibling(self.mine.at[0])

    def near(self):
        for i, k in enumerate((1, 7)):
            wait_bytes(self.mine.at[k], self.near_recv.at[i])
            self.to_sibling(self.mine.at[k])

    def finish(self):
        wait_bytes(self.w.at[1 - self.p.c], self.sib_recv)

    def drain(self):
        super().drain()
        wait_bytes(self.mine.at[pl.ds(2, 5), 0], self.s1_send)
        wait_bytes(self.mine.at[pl.ds(1, 2)], self.near_send)
        wait_bytes(self.mine, self.sib_send)


class RowGather(Gather):
    def __init__(self, place, source, held, straight, sems):
        self.source, self.held = source, held
        self.s1_send, self.s1_recv = sems[:2]
        super().__init__(
            place,
            lambda e: held.at[place.c, e],
            lambda e, s: held.at[place.c, e, :, pl.ds(s * 1024, 1024)],
            held.at[place.c, pl.ds(0, 15)],
            straight,
            sems[2:],
        )

    def start(self):
        p = self.p
        dst = self.held.at[p.c, p.d, :, pl.ds(pl.multiple_of(p.z * COLS, COLS), COLS)]
        pltpu.make_async_copy(self.source, dst, self.s1_recv).start()
        for k in (4, 3, 5, 2, 6, 1, 7):
            z = lax.rem(p.z + k, 8)
            remote(self.source, dst, self.s1_send, self.s1_recv, (p.d, z * 2 + p.c)).start()

    def own(self):
        wait_bytes(self.block(self.p.d), self.s1_recv)
        super().own()

    def finish(self):
        wait_bytes(self.held.at[1 - self.p.c], self.sib_recv)

    def drain(self):
        super().drain()
        wait_bytes(self.held.at[0, 0, :, pl.ds(0, 7 * COLS)], self.s1_send)
        wait_bytes(self.held.at[self.p.c], self.sib_send)


def all_to_all(place, source, target, send_sem, recv_sem):
    p = place

    def one(k, carry):
        g = lax.rem(p.f + k, NF)
        remote(source(g), target(p.f), send_sem, recv_sem, (p.d, g)).start()
        return carry

    pltpu.make_async_copy(source(p.f), target(p.f), recv_sem).start()
    lax.fori_loop(1, NF, one, 0)


def mean_square(rows):
    return jnp.mean(rows * rows, axis=-1, keepdims=True)


def kernel(
    lengths, partner, stream_hbm, norm_hbm, wq_hbm, wk_hbm, wv_hbm, wo_hbm, q_gain, k_gain, final_hbm,
    cos_hbm, sin_hbm,
    grad_out, loss_out,
    norm_gain, final_gain, stream, normed, gain_row, wk, wv, everyone, wq, wo, cos_t, sin_t,
    pool_send, pool_recv, q_send, q_recv, mix_send, mix_recv, mix_f32,
    ab_send, ab_recv, c_send, c_recv, u_send, keys, values, sim,
    load_sem, pair_sem,
    k0, k1, k2, k3, k4, k5, k6, k7, k8, k9,
    v0, v1, v2, v3, v4, v5, v6, v7, v8, v9,
    u0, u1, u2, u3, u4, u5, u6,
):
    p = Place()
    d, f = p.d, p.f
    rows_of = lambda g, n: pl.ds(pl.multiple_of(g * n, n), n)
    lanes_of = lambda g, n: pl.ds(pl.multiple_of(g * n, n), n)

    quarter = TOKENS // 4
    loads = [
        pltpu.make_async_copy(stream_hbm.at[pl.ds(i * quarter, quarter)], stream.at[pl.ds(i * quarter, quarter)], load_sem.at[i])
        for i in range(4)
    ]
    loads += [
        pltpu.make_async_copy(norm_hbm, norm_gain, load_sem.at[7]),
        pltpu.make_async_copy(final_hbm, final_gain, load_sem.at[8]),
        pltpu.make_async_copy(wq_hbm, wq, load_sem.at[4]),
        pltpu.make_async_copy(cos_hbm, cos_t, load_sem.at[5]),
        pltpu.make_async_copy(sin_hbm, sin_t, load_sem.at[6]),
    ]
    for load in loads:
        load.start()

    barrier = pltpu.get_barrier_semaphore()

    def greet(k, carry):
        pl.semaphore_signal(barrier, inc=1, device_id=(d, lax.rem(f + k, NF)), device_id_type=pl.DeviceIdType.MESH)
        pl.semaphore_signal(barrier, inc=1, device_id=(lax.rem(d + k, ND), f), device_id_type=pl.DeviceIdType.MESH)
        return carry

    lax.fori_loop(1, NF, greet, 0)
    pl.semaphore_wait(barrier, NF - 1 + ND - 1)

    k_gather = WeightGather(p, wk_hbm, wk, K_STRAIGHT, (k0, k1, k2, k3, k4, k5, k6, k7, k8, k9))
    v_gather = WeightGather(p, wv_hbm, wv, V_STRAIGHT, (v0, v1, v2, v3, v4, v5, v6, v7, v8, v9))
    u_gather = RowGather(p, u_send, everyone, U_STRAIGHT, (u0, u1, u2, u3, u4, u5, u6))

    k_gather.start()

    for load in loads[:5]:
        load.wait()
    last = lengths[0, 0] - 1
    gain = norm_gain[...].astype(F32).reshape(1, WIDTH)
    for t in range(2):
        if t == 0:
            row = jnp.zeros((16, WIDTH), F32)
            for start in range(LEAST_LAST // 16 * 16, MOST_LAST + 1, 16):
                here = lax.broadcasted_iota(jnp.int32, (16, WIDTH), 0) == last - start
                row += jnp.where(here, stream[pl.ds(start, 16), :].astype(F32), 0.0)
            row = jnp.sum(row, axis=0, keepdims=True)
        else:
            row = stream[pl.ds(TOKENS - 16, 16), :].astype(F32)[15:16]
        norm_row = (row * lax.rsqrt(mean_square(row) + EPS) * gain).astype(BF16).astype(F32)
        for g in range(NF):
            for h in range(2):
                lane = g * COLS + h * 128
                pool_send[pl.ds(g * 8 + t * 2 + h, 1), :] = norm_row[:, lane : lane + 128]
                pool_send[pl.ds(g * 8 + 4 + t * 2 + h, 1), :] = row[:, lane : lane + 128]
    all_to_all(
        p, lambda g: pool_send.at[rows_of(g, 8)], lambda g: pool_recv.at[rows_of(g, 8)], pair_sem.at[0], pair_sem.at[1]
    )
    v_gather.start()
    k_gather.start_near()
    gain_row[...] = gain

    def norm_rows(i, carry):
        rows = pl.ds(pl.multiple_of(i * 32, 32), 32)
        block = stream[rows, :].astype(F32)
        inverse = lax.rsqrt(mean_square(block) + EPS)
        for k in range(8):
            lanes = lanes_of(lax.rem(p.z + k, 8), 2 * COLS)
            chunk = (stream[rows, lanes].astype(F32) * inverse * gain_row[:, lanes]).astype(BF16)
            for core in range(2):
                normed[core, rows, k * COLS : k * COLS + COLS] = chunk[:, core * COLS : core * COLS + COLS]
        return carry

    lax.fori_loop(0, TOKENS // 32, norm_rows, 0)

    k_gather.own()

    for load in loads[5:]:
        load.wait()
    wait_bytes(pool_recv, pair_sem.at[1])

    def pooled_block(first):
        return jnp.concatenate(
            [
                jnp.concatenate([pool_recv[pl.ds(first + t * 2 + h, NF, stride=8), :] for h in range(2)], axis=1)
                for t in range(2)
            ],
            axis=0,
        )

    shares = jnp.dot(pooled_block(0).astype(BF16), wq[...], preferred_element_type=F32)
    for t in range(2):
        for h in range(QUERY_HEADS):
            q_send[pl.ds(t * 16 + h, NF, stride=32), :] = shares[t * 16 : t * 16 + 16, h * 128 : h * 128 + 128]
    all_to_all(
        p, lambda g: q_send.at[rows_of(g, 32)], lambda g: q_recv.at[rows_of(g, 32)], pair_sem.at[2], pair_sem.at[3]
    )

    k_gather.first_near()
    v_gather.own()
    v_gather.start_near()
    k_gather.own_shard()
    k_gather.first_far()

    def wo_rows(core):
        return pl.ds(pl.multiple_of((p.x * (1 - core) + p.y * core) * 32, 32), 32)

    def send_wo(k, carry):
        g = lax.rem(f + k, NF)
        rows = wo_rows(g % 2)
        remote(wo_hbm.at[rows, lanes_of(g, COLS)], wo.at[f, rows], pair_sem.at[4], pair_sem.at[5], (d, g)).start()
        return carry

    pltpu.make_async_copy(wo_hbm.at[wo_rows(p.c), lanes_of(f, COLS)], wo.at[f, wo_rows(p.c)], pair_sem.at[5]).start()
    lax.fori_loop(1, NF, send_wo, 0)

    k_gather.second_near((0,))
    v_gather.first_near()
    k_gather.second_near((3, 1))
    v_gather.own_shard()
    v_gather.first_far()
    k_gather.second_near((2,))
    k_gather.near()
    v_gather.second_near((0,))
    k_gather.second_far()

    key_gain = k_gain[...].astype(F32)

    def half_product(w, core, rows):
        return jnp.dot(
            normed[core, rows, :],
            w[core].reshape(WIDTH // 2, 512),
            preferred_element_type=F32,
        )

    def first_half(w):
        for i in range(2):
            rows = pl.ds(i * 256, 256)
            sim[rows, :] = half_product(w, p.c, rows)

    first_half(wk)
    k_gather.finish()
    for i in range(2):
        rows = pl.ds(i * 256, 256)
        sim[rows, :] += half_product(wk, 1 - p.c, rows)
    v_gather.second_near((3, 1))

    def key_rows(i, carry):
        rows = pl.ds(pl.multiple_of(i * 128, 128), 128)
        for g in range(KEY_VALUE_HEADS):
            one = sim[rows, g * 128 : g * 128 + 128]
            one = one * lax.rsqrt(mean_square(one) + EPS) * key_gain
            one = one * cos_t[rows, :] + pltpu.roll(one, 64, 1) * sin_t[rows, :]
            keys[rows, g * 128 : g * 128 + 128] = one.astype(BF16)
        return carry

    lax.fori_loop(0, TOKENS // 128, key_rows, 0)
    wait_bytes(q_recv, pair_sem.at[3])
    query = q_recv[pl.ds(0, 32), :]
    for g in range(1, NF):
        query += q_recv[pl.ds(g * 32, 32), :]
    query = query * lax.rsqrt(mean_square(query) + EPS) * q_gain[...].astype(F32)
    row32 = lax.broadcasted_iota(jnp.int32, (32, 128), 0)

    def pooled_angle(table):
        start = LEAST_LAST // 8 * 8
        rows = table[pl.ds(start, MOST_LAST + 1 - start), :]
        here = lax.broadcasted_iota(jnp.int32, rows.shape, 0) == last - start
        first = jnp.sum(jnp.where(here, rows, 0.0), axis=0, keepdims=True)
        return jnp.where(row32 < 16, first, table[pl.ds(TOKENS - 1, 1), :])

    query = query * pooled_angle(cos_t) + pltpu.roll(query, 64, 1) * pooled_angle(sin_t)
    group = row32 % 16 // 4
    q_block = jnp.concatenate(
        [jnp.where(group == g, query, 0.0) for g in range(KEY_VALUE_HEADS)], axis=1
    ).astype(BF16)

    scores = lax.dot_general(q_block, keys[...], (((1,), (1,)), ((), ())), preferred_element_type=F32)
    scores = scores * (1.0 / math.sqrt(HEAD_SIZE))
    token = lax.broadcasted_iota(jnp.int32, scores.shape, 1)
    first_text = lax.broadcasted_iota(jnp.int32, scores.shape, 0) < 16
    inside = (token < lengths[0, 0]) == first_text
    weights = jnp.where(inside, jnp.exp(scores), 0.0)
    probs = (weights / jnp.sum(weights, axis=1, keepdims=True)).astype(BF16)

    v_gather.second_near((2,))
    v_gather.near()
    v_gather.second_far()
    own_wo = wo.at[:, wo_rows(p.c)]
    wait_bytes(own_wo, pair_sem.at[5])
    for k in (1, 3, 2):
        remote(own_wo, own_wo, pair_sem.at[12], pair_sem.at[13], (p.index(k, 0), f)).start()

    first_half(wv)
    v_gather.finish()
    for i in range(2):
        rows = pl.ds(i * 256, 256)
        values[rows, :] = (sim[rows, :] + half_product(wv, 1 - p.c, rows)).astype(BF16)
    all_mixed = jnp.dot(probs, values[...], preferred_element_type=F32)
    mixed = jnp.zeros((32, 128), F32)
    for g in range(KEY_VALUE_HEADS):
        mixed += jnp.where(group == g, all_mixed[:, g * 128 : g * 128 + 128], 0.0)
    mix_send[...] = mixed.astype(BF16)
    all_to_all(p, lambda g: mix_send, lambda g: mix_recv.at[g], pair_sem.at[6], pair_sem.at[7])
    wait_bytes(wo.at[pl.ds(0, 12)], pair_sem.at[13])
    wait_bytes(mix_recv, pair_sem.at[7])

    mix_f32[...] = mix_recv[...].astype(F32).reshape(NF * 32, 128)
    wide = jnp.concatenate(
        [
            jnp.concatenate([mix_f32[pl.ds(t * 16 + h, NF, stride=32), :] for h in range(QUERY_HEADS)], axis=1)
            for t in range(2)
        ],
        axis=0,
    ).astype(BF16)
    state = pooled_block(4) + jnp.dot(wide, wo[...].reshape(2048, COLS), preferred_element_type=F32)
    gained = state * final_gain[lanes_of(f, COLS)].astype(F32).reshape(1, COLS)
    u_send[...] = gained.astype(BF16)
    u_gather.start()

    offset = d % 4 * 32
    row = lax.broadcasted_iota(jnp.int32, (32, 128), 0)
    lane = lax.broadcasted_iota(jnp.int32, (32, 128), 1)
    diagonal = lane == row + offset
    as_lanes = lambda column: jnp.sum(jnp.where(diagonal, column, 0.0), axis=0, keepdims=True)
    square = as_lanes(jnp.sum(state * state, axis=1, keepdims=True))
    gained_square = as_lanes(jnp.sum(gained * gained, axis=1, keepdims=True))
    lane1 = lax.broadcasted_iota(jnp.int32, (1, 128), 1)
    own = [partner[0, 0], partner[0, 1]]
    partners = jnp.where(lane1 == offset + f, own[0], 0) + jnp.where(lane1 == offset + 16 + f, own[1], 0)
    row8 = lax.broadcasted_iota(jnp.int32, (8, 128), 0)
    pack = lambda parts: functools.reduce(
        lambda total, item: jnp.where(row8 == item[0], item[1], total), enumerate(parts), jnp.zeros((8, 128), F32)
    )
    ab_send[...] = pack([square, gained_square, partners.astype(F32)])
    all_to_all(p, lambda g: ab_send, lambda g: ab_recv.at[rows_of(g, 8)], pair_sem.at[8], pair_sem.at[9])
    u_gather.own()

    wait_bytes(ab_recv, pair_sem.at[9])
    sums = ab_recv[pl.ds(0, 8), :]
    for g in range(1, NF):
        sums += ab_recv[pl.ds(g * 8, 8), :]
    inverse = lax.rsqrt(sums[0:1] / WIDTH + EPS)
    factor = inverse * lax.rsqrt(inverse * inverse * sums[1:2] + EPS)
    factor = jnp.where((lane1 >= offset) & (lane1 < offset + 32), factor, 0.0)
    c_send[...] = pack([factor, sums[2:3]])

    def send_factor(k, carry):
        e = lax.rem(d + k, ND)
        remote(c_send, c_recv.at[rows_of(d, 8)], pair_sem.at[10], pair_sem.at[11], (e, f)).start()
        return carry

    pltpu.make_async_copy(c_send, c_recv.at[rows_of(d, 8)], pair_sem.at[11]).start()
    lax.fori_loop(1, ND, send_factor, 0)

    k_gather.drain()
    v_gather.drain()
    wait_bytes(pool_send.at[pl.ds(0, 15 * 8)], pair_sem.at[0])
    wait_bytes(q_send.at[pl.ds(0, 15 * 32)], pair_sem.at[2])
    wait_bytes(wo.at[pl.ds(0, 15), pl.ds(0, 32)], pair_sem.at[4])
    wait_bytes(wo.at[pl.ds(0, 12)], pair_sem.at[12])
    wait_bytes(mix_recv.at[pl.ds(0, 15)], pair_sem.at[6])

    u_gather.first_near()
    u_gather.first_far()
    u_gather.second_near()
    u_gather.second_far()
    wait_bytes(c_recv, pair_sem.at[11])
    folded = []
    for q in range(4):
        folded.append(sum(c_recv[pl.ds((q * 4 + i) * 8, 8), :] for i in range(1, 4)) + c_recv[pl.ds(q * 32, 8), :])
    factor_row = jnp.concatenate([block[0:1] for block in folded], axis=1)
    partner_row = jnp.concatenate([block[1:2] for block in folded], axis=1).astype(jnp.int32)
    square_row = lax.broadcasted_iota(jnp.int32, (128, 128), 0)
    square_lane = lax.broadcasted_iota(jnp.int32, (128, 128), 1)
    factor_column = [
        jnp.sum(jnp.where(square_row == square_lane, block[0:1], 0.0), axis=1, keepdims=True) for block in folded
    ]

    def half_scores(core, i):
        return lax.dot_general(
            everyone[core, pl.ds(i * 8, 8)].reshape(256, WIDTH // 2),
            everyone[core].reshape(TEXTS, WIDTH // 2),
            (((1,), (1,)), ((), ())),
            preferred_element_type=F32,
        )

    for i in range(2):
        sim[pl.ds(i * 256, 256), :] = half_scores(p.c, i)
    u_gather.finish()
    name_of = lambda j: j // 32 * 32 + j % 16 * 2 + j % 32 // 16
    total = jnp.zeros((1, TEXTS), F32)
    target = jnp.zeros((1, TEXTS), F32)
    for i in range(2):
        rows = pl.ds(i * 256, 256)
        block = sim[rows, :] + half_scores(1 - p.c, i)
        column = jnp.concatenate(factor_column[i * 2 : i * 2 + 2], axis=0) * (1.0 / TEMPER)
        block = block * column * factor_row
        sim[rows, :] = block
        i_index = lax.broadcasted_iota(jnp.int32, block.shape, 0) + i * 256
        j_index = lax.broadcasted_iota(jnp.int32, block.shape, 1)
        hit = name_of(i_index) == partner_row
        total += jnp.sum(jnp.where((i_index != j_index) | hit, jnp.exp(block), 0.0), axis=0, keepdims=True)
        target += jnp.sum(jnp.where(hit, block, 0.0), axis=0, keepdims=True)
    loss_out[...] = jnp.sum(jnp.log(total) - target, axis=1, keepdims=True) * (1.0 / TEXTS)

    j_index = lax.broadcasted_iota(jnp.int32, (1, TEXTS), 1)
    names = name_of(j_index)
    coefficient = []
    for t in range(2):
        place = d * 32 + t * 16 + f
        name = (d * NF + f) * 2 + t
        exps = jnp.exp(sim[pl.ds(place, 1), :])
        own_total = jnp.sum(jnp.where(j_index == place, total, 0.0), axis=1, keepdims=True)
        other = j_index != place
        hit = names == own[t]
        back = partner_row == name
        pull = jnp.where(other | hit, exps, 0.0) / own_total - hit.astype(F32)
        pulled = jnp.where(other | back, exps, 0.0) / total - back.astype(F32)
        coefficient.append((pull.astype(BF16).astype(F32) + pulled.astype(BF16).astype(F32)) * factor_row)
    high = [item.astype(BF16).astype(F32) for item in coefficient]
    low = [item - part for item, part in zip(coefficient, high)]
    row16 = lax.broadcasted_iota(jnp.int32, (16, TEXTS), 0)
    stack = jnp.zeros((16, TEXTS), F32)
    for n, item in enumerate(high + low):
        stack = jnp.where(row16 == n, item, stack)
    stack = stack.astype(BF16)
    for core in range(2):
        for n in range(2):
            part = jnp.dot(
                stack, everyone[core, :, :, n * 1024 : n * 1024 + 1024].reshape(TEXTS, 1024), preferred_element_type=F32
            )
            part = (part[0:2] + part[2:4]) * (1.0 / TEMPER)
            for m in range(4):
                lane = ((n * 4 + m) * 2 + core) * COLS
                grad_out[:, lane : lane + COLS] = part[:, m * COLS : m * COLS + COLS]

    u_gather.drain()
    wait_bytes(ab_recv.at[pl.ds(0, 15 * 8)], pair_sem.at[8])
    wait_bytes(c_recv.at[pl.ds(0, 15 * 8)], pair_sem.at[10])


def local(
    stream, lengths, partner, norm_gain, w_query, key_weight, value_weight, w_out, q_gain, key_norm_gain, final_gain
):
    cos_table, sin_table = rotary_tables()
    vmem = pl.BlockSpec(memory_space=pltpu.VMEM)
    smem = pl.BlockSpec(memory_space=pltpu.SMEM)
    hbm = pl.BlockSpec(memory_space=pltpu.HBM)
    dma = pltpu.SemaphoreType.DMA
    plane_sems = [dma, dma, dma, dma((4,)), dma((4, 4))]
    weight_sems = [dma, dma, dma, dma((2,)), dma] + plane_sems
    grad, loss = pl.pallas_call(
        kernel,
        out_shape=(
            jax.ShapeDtypeStruct((2, WIDTH), F32),
            jax.ShapeDtypeStruct((1, 1), F32),
        ),
        in_specs=[smem, smem, hbm, hbm, hbm, hbm, hbm, hbm, vmem, vmem, hbm, hbm, hbm],
        out_specs=(vmem, vmem),
        scratch_shapes=[
            pltpu.VMEM((WIDTH,), BF16),
            pltpu.VMEM((WIDTH,), BF16),
            pltpu.VMEM((TOKENS, WIDTH), BF16),
            pltpu.VMEM((2, TOKENS, WIDTH // 2), BF16),
            pltpu.VMEM((1, WIDTH), F32),
            pltpu.VMEM((2, 8, ND, 16, 512), BF16),
            pltpu.VMEM((2, 8, ND, 16, 512), BF16),
            pltpu.VMEM((2, ND, 32, WIDTH // 2), BF16),
            pltpu.VMEM((COLS, 2048), BF16),
            pltpu.VMEM((NF, 128, COLS), BF16),
            pltpu.VMEM((TOKENS, HEAD_SIZE), F32),
            pltpu.VMEM((TOKENS, HEAD_SIZE), F32),
            pltpu.VMEM((NF * 8, 128), F32),
            pltpu.VMEM((NF * 8, 128), F32),
            pltpu.VMEM((NF * 32, 128), F32),
            pltpu.VMEM((NF * 32, 128), F32),
            pltpu.VMEM((32, 128), BF16),
            pltpu.VMEM((NF, 32, 128), BF16),
            pltpu.VMEM((NF * 32, 128), F32),
            pltpu.VMEM((8, 128), F32),
            pltpu.VMEM((NF * 8, 128), F32),
            pltpu.VMEM((8, 128), F32),
            pltpu.VMEM((ND * 8, 128), F32),
            pltpu.VMEM((32, COLS), BF16),
            pltpu.VMEM((TOKENS, 512), BF16),
            pltpu.VMEM((TOKENS, 512), BF16),
            pltpu.VMEM((TEXTS, TEXTS), F32),
            dma((11,)),
            dma((14,)),
        ]
        + weight_sems * 2
        + [dma, dma]
        + plane_sems,
        compiler_params=pltpu.CompilerParams(
            collective_id=0, has_side_effects=True, vmem_limit_bytes=60 * 1024 * 1024
        ),
    )(
        lengths,
        partner.reshape(1, 2),
        stream,
        norm_gain,
        w_query,
        key_weight.reshape(ND, 16, 512),
        value_weight.reshape(ND, 16, 512),
        w_out,
        q_gain.reshape(1, HEAD_SIZE),
        key_norm_gain.reshape(1, HEAD_SIZE),
        final_gain,
        jnp.asarray(cos_table),
        jnp.asarray(sin_table),
    )
    return (grad, loss.reshape(()))


def solution(mesh):
    return jax.shard_map(
        local,
        mesh=mesh,
        in_specs=(
            P(("dp", "fsdp"), None),
            P(("dp", "fsdp"), None),
            P(("dp", "fsdp")),
            P(),
            P("fsdp", None),
            P("fsdp", None),
            P("fsdp", None),
            P("fsdp", None),
            P(),
            P(),
            P(),
        ),
        out_specs=(P(("dp", "fsdp"), None), P()),
        check_vma=False,
    )
```
